128 devices in a mesh: grp: 16 (over x, y), tp: 8 (over z, core).
Axes of the slice: x: 4, y: 4, z: 4, core: 2. Of those that a mesh axis runs over, the one named last changes fastest.
Arguments:
- sel_hidden: bfloat16 [32, 320, 4096], P('grp'), may hold values from -6 to 6
- norm_gain: float32 [4096], replicated, may hold values from 0.25 to 1.75
- w_query: bfloat16 [4096, 4096], P(None, 'tp'), may hold values from -0.09375 to 0.09375
- w_key: bfloat16 [4096, 1024], P(None, 'tp'), may hold values from -0.1875 to 0.1875
- w_value: bfloat16 [4096, 1024], P(None, 'tp'), may hold values from -0.09375 to 0.09375
- w_out: bfloat16 [4096, 4096], P(None, 'tp'), may hold values from -0.09375 to 0.09375
- doc_cache: bfloat16 [256, 2, 512, 1024], P('grp', None, None, 'tp'), may hold values from -250 to 250
- home: int32 [256], replicated, may hold values from 0 to 255, as said below
- doc_ids: int32 [32, 8], replicated, may hold values from 0 to 255, as said below
- doc_len: int32 [256], replicated, may hold values from 128 to 512, as said below
- positions: int32 [32, 320], P('grp'), may hold values from 0 to 4095, as said below
Outputs:
- mixed: bfloat16 [32, 320, 4096], P('grp', None, 'tp')
The draws below stay inside these ranges and needn't reach their ends.
Inputs may be any that keep to these rules, and one draw needn't show every extreme that they name: `home`: a permutation: every location holds one document; the owner of location l along grp is l // 16. `doc_ids`: requests g * 2 .. (g + 1) * 2 - 1 form serving group g; the 16 documents of one group all differ, no owner holds more than 2 of them, and in every group at least one owner holds exactly 2. `doc_len`: documents doc_ids[0, 0] and doc_ids[0, 7] have length 512 (others may too). positions: each row rises; for each j it holds 40 positions j * 512 + t with t below the length of document doc_ids[r, j].
All inputs are finite; a program needn't handle non-finite values.
Results may differ from the reference program's by a relative error of at most 0.006.
The reference program's roundings to bfloat16 on the way (of `normed`, `weights` and `attn`) count: a program that leaves them out, or rounds other values in their place, can miss the bound.
Values may be sent and summed in bfloat16 or wider, within the bound.
No kernel may reach another device: no remote copies, remote signals or barrier semaphores. Data moves between devices by JAX's collectives and lax.ppermute only.
A program may use at most 192 MiB of HBM per device.

```python
import jax
import jax.numpy as jnp
from jax import lax

D = 4096
H = 32
KVH = 8
HD = 128
R_DOCS = 8
DOC_LEN = 512
CAP = 2
REQ_GRP = 2
PICK = 40
DOC_DEV = 16
RECOMP = 320
REQS = 32
DOCS = 256


def plan_tables(key):
    keys = jax.random.split(key, 8)
    groups = REQS // REQ_GRP
    per_group = REQ_GRP * R_DOCS
    home = jax.random.permutation(keys[0], DOCS).astype(jnp.int32)
    resident = jnp.argsort(home).astype(jnp.int32)
    first = jax.random.randint(keys[1], (groups,), 0, groups)
    spread = (groups - 1) * CAP
    tickets = jax.random.randint(keys[2], (groups, spread), 0, 2 ** 20) * spread + jnp.arange(spread)[None, :]
    order = jnp.argsort(tickets, axis=1)[:, :per_group - CAP]
    others = (first[:, None] + 1 + order // CAP) % groups
    owners = jnp.concatenate([jnp.broadcast_to(first[:, None], (groups, CAP)), others], axis=1)
    within = jnp.concatenate([jnp.broadcast_to(jnp.arange(CAP)[None, :], (groups, CAP)), order % CAP], axis=1)
    span = DOC_DEV // CAP
    lower = jnp.minimum(jax.random.randint(keys[3], (groups, per_group), 0, span), jax.random.randint(keys[4], (groups, per_group), 0, span))
    location = owners * DOC_DEV + within * span + lower
    shuffle = jnp.argsort(jax.random.randint(keys[5], (groups, per_group), 0, 2 ** 20) * per_group + jnp.arange(per_group)[None, :], axis=1)
    location = jnp.take_along_axis(location, shuffle, axis=1).reshape(REQS, R_DOCS)
    doc_ids = resident[location].astype(jnp.int32)
    lengths = jax.random.randint(keys[6], (DOCS,), DOC_LEN // 4, DOC_LEN + 1)
    lengths = lengths.at[doc_ids[0, 0]].set(DOC_LEN)
    lengths = lengths.at[doc_ids[0, R_DOCS - 1]].set(DOC_LEN)
    lengths = lengths.at[doc_ids[0, 1]].set(DOC_LEN // 4).astype(jnp.int32)
    own_len = lengths[doc_ids]
    offsets = jnp.arange(DOC_LEN)
    marks = jax.random.randint(keys[7], (REQS, R_DOCS, DOC_LEN), 0, 2 ** 20) * DOC_LEN + offsets
    marks = jnp.where(offsets[None, None, :] < own_len[:, :, None], marks, 2 ** 30)
    req_ix = jnp.arange(REQS)[:, None, None]
    doc_ix = jnp.arange(R_DOCS)[None, :, None]
    off_ix = offsets[None, None, :]
    forced = (req_ix == 0) & ((doc_ix == 0) & (off_ix == 0) | (doc_ix == R_DOCS - 1) & (off_ix == DOC_LEN - 1))
    marks = jnp.where(forced, -1, marks)
    picked = jnp.sort(jnp.argsort(marks, axis=2)[:, :, :PICK], axis=2)
    rows = (picked + jnp.arange(R_DOCS)[None, :, None] * DOC_LEN).reshape(REQS, RECOMP).astype(jnp.int32)
    return (home, doc_ids, lengths, rows)


def draw_home(key, part):
    return plan_tables(key)[0]


def draw_doc_ids(key, part):
    return plan_tables(key)[1]


def draw_doc_len(key, part):
    return plan_tables(key)[2]


def draw_positions(key, part):
    return plan_tables(key)[3]


def draw_doc_cache(key, part):
    key = jax.random.fold_in(key, 11)
    key_k, key_v = jax.random.split(key, 2)
    shape = (DOCS, DOC_LEN, KVH * HD)
    cached_keys = jnp.clip(2.0 * jax.random.normal(key_k, shape), -12.0, 12.0)
    cached_values = jnp.clip(jax.random.normal(key_v, shape), -6.0, 6.0)
    return jnp.stack([cached_keys, cached_values], axis=1).astype(jnp.bfloat16)


def shard_levels(key, shape, pieces, least, high):
    loudness, own = 1.0, jax.random.fold_in(key, 6)
    for axis_at, blocks in pieces:
        steps = jnp.exp(jax.random.uniform(jax.random.fold_in(own, axis_at), (blocks,), jnp.float32, least / len(pieces), high / len(pieces)))
        loudness = loudness * jnp.repeat(steps, shape[axis_at] // blocks).reshape([-1 if axis == axis_at else 1 for axis in range(len(shape))])
    return loudness


def gaussian(own_key, dims, deviation, bound, cuts=(), held_as=jnp.bfloat16):
    entries = deviation * jax.random.normal(own_key, dims, jnp.float32)
    if cuts:
        entries = entries * shard_levels(own_key, dims, cuts, -0.22, 0.18)
    return jnp.clip(entries, -bound, bound).astype(held_as)


def setup_inputs(seed: int = 0) -> dict:
    splits = jax.random.split(jax.random.key(seed), 12)
    sel_hidden = gaussian(splits[0], (REQS, RECOMP, D), 1.0, 6.0, ((0, 16),))
    norm_gain = jnp.clip(1.0 + 0.15 * jax.random.normal(splits[1], (D,), jnp.float32), 0.25, 1.75)
    w_query = gaussian(splits[2], (D, H * HD), D ** -0.5, 0.09375, ((1, 8),))
    w_key = gaussian(splits[3], (D, KVH * HD), (D // 4) ** -0.5, 0.1875, ((1, 8),))
    w_value = gaussian(splits[4], (D, KVH * HD), D ** -0.5, 0.09375, ((1, 8),))
    w_out = gaussian(splits[5], (H * HD, D), (H * HD) ** -0.5, 0.09375, ((1, 8),))
    doc_cache = draw_doc_cache(jax.random.fold_in(splits[11], 71), 0)
    home = draw_home(jax.random.fold_in(splits[11], 71), 0)
    doc_ids = draw_doc_ids(jax.random.fold_in(splits[11], 71), 0)
    doc_len = draw_doc_len(jax.random.fold_in(splits[11], 71), 0)
    positions = draw_positions(jax.random.fold_in(splits[11], 71), 0)
    return dict(sel_hidden=sel_hidden, norm_gain=norm_gain, w_query=w_query, w_key=w_key, w_value=w_value, w_out=w_out, doc_cache=doc_cache, home=home, doc_ids=doc_ids, doc_len=doc_len, positions=positions)


def reference(sel_hidden, norm_gain, w_query, w_key, w_value, w_out, doc_cache, home, doc_ids, doc_len, positions):
    group = H // KVH
    scale = HD ** (-0.5)

    def one_request(items):
        hidden, ids, where_rows = items
        xf = hidden.astype(jnp.float32)
        normed = (xf * lax.rsqrt(lax.optimization_barrier(jnp.mean(xf * xf, axis=-1, keepdims=True)) + 1e-05) * norm_gain).astype(jnp.bfloat16)
        query = jnp.dot(normed, w_query, preferred_element_type=jnp.float32).astype(jnp.bfloat16)
        key_new = jnp.dot(normed, w_key, preferred_element_type=jnp.float32).astype(jnp.bfloat16)
        value_new = jnp.dot(normed, w_value, preferred_element_type=jnp.float32).astype(jnp.bfloat16)
        context = doc_cache[home[ids]]
        keys_ctx = context[:, 0].reshape(R_DOCS * DOC_LEN, KVH * HD).at[where_rows].set(key_new)
        values_ctx = context[:, 1].reshape(R_DOCS * DOC_LEN, KVH * HD).at[where_rows].set(value_new)
        lengths = doc_len[ids]
        valid = (jnp.arange(DOC_LEN, dtype=jnp.int32)[None, :] < lengths[:, None]).reshape(R_DOCS * DOC_LEN)
        visible = valid[None, :] & (jnp.arange(R_DOCS * DOC_LEN, dtype=jnp.int32)[None, :] <= where_rows[:, None])

        def one_head(head):
            keys_h = lax.dynamic_slice_in_dim(keys_ctx, head * HD, HD, 1).astype(jnp.float32)
            values_h = lax.dynamic_slice_in_dim(values_ctx, head * HD, HD, 1).astype(jnp.float32)
            query_h = lax.dynamic_slice_in_dim(query, head * group * HD, group * HD, 1).reshape(RECOMP, group, HD).astype(jnp.float32)
            scores = jnp.einsum('qgd,kd->gqk', query_h, keys_h) * scale
            scores = jnp.where(visible[None], scores, -1e+30)
            top = lax.optimization_barrier(jnp.max(scores, axis=-1, keepdims=True))
            expo = jnp.exp(scores - top)
            weights = (expo / lax.optimization_barrier(jnp.sum(expo, axis=-1, keepdims=True))).astype(jnp.bfloat16)
            attn = jnp.einsum('gqk,kd->qgd', weights.astype(jnp.float32), values_h).astype(jnp.bfloat16)
            return attn.reshape(RECOMP, group * HD)
        heads = lax.map(one_head, jnp.arange(KVH, dtype=jnp.int32))
        attn_all = jnp.transpose(heads, (1, 0, 2)).reshape(RECOMP, H * HD)
        return jnp.dot(attn_all, w_out, preferred_element_type=jnp.float32).astype(jnp.bfloat16)
    return lax.map(one_request, (sel_hidden, doc_ids, positions))
```

```python
import functools
import math

import jax
import jax.numpy as jnp
from jax import lax
from jax.experimental import pallas as pl
from jax.experimental.pallas import tpu as pltpu
from jax.sharding import PartitionSpec as P

H = 32
KVH = 8
HD = 128
CAP = 2
GROUP = H // KVH
SIDE = 4
GROUPS = 16
DOC = 512
TOKENS = 320
RETRIEVED = 8
TILES = 4
SUB = TOKENS // TILES
ROWS = SUB * GROUP
PADDED = 384
FAR = 2**30
EXP2 = HD ** (-0.5) * math.log2(math.e)

NEAR = [(1, 0), (3, 0), (0, 1), (0, 3)]
DIAGONAL = [(1, 1), (3, 3), (1, 3), (3, 1)]
TWO = [(2, 0), (0, 2)]
OPPOSITE = [(2, 2)]
KNIGHT = {(0, 1): (2, 1), (0, 3): (2, 3), (1, 0): (1, 2), (3, 0): (3, 2)}
SHIFTS = NEAR + DIAGONAL + TWO + OPPOSITE + [KNIGHT[s] for s in NEAR]

ANY = pl.BlockSpec(memory_space=pl.ANY)
VMEM = pl.BlockSpec(memory_space=pltpu.VMEM)
SMEM = pl.BlockSpec(memory_space=pltpu.SMEM)


def shift(block, by):
    pairs = [
        (x * SIDE + y, (x + by[0]) % SIDE * SIDE + (y + by[1]) % SIDE)
        for x in range(SIDE)
        for y in range(SIDE)
    ]
    return lax.ppermute(block, "grp", pairs)


def pack_kernel(me_ref, chosen_ref, cache_ref, *refs):
    out_refs, sem = refs[: len(SHIFTS)], refs[len(SHIFTS)]
    me = me_ref[0]
    x, y = me // SIDE, me % SIDE

    def each(act):
        for (dx, dy), out in zip(SHIFTS, out_refs):
            g = (x + dx) % SIDE * SIDE + (y + dy) % SIDE
            for k in range(CAP):
                doc = chosen_ref[g * CAP + k]

                @pl.when(doc >= 0)
                def _():
                    act(pltpu.make_async_copy(cache_ref.at[doc], out.at[k], sem))

    each(lambda copy: copy.start())
    each(lambda copy: copy.wait())


def pack(me, chosen, cache):
    return pl.pallas_call(
        pack_kernel,
        out_shape=[jax.ShapeDtypeStruct((CAP, 2, DOC, HD), jnp.bfloat16)] * len(SHIFTS),
        in_specs=[SMEM, SMEM, ANY],
        out_specs=[ANY] * len(SHIFTS),
        scratch_shapes=[pltpu.SemaphoreType.DMA],
        cost_estimate=pl.CostEstimate(flops=0, bytes_accessed=10 << 20, transcendentals=0),
        name="pack",
    )(me, chosen, cache)


def attend_kernel(counts, first, last, table_ref, q_ref, pos_ref, idx_ref, *refs):
    refs = list(refs)
    if first:
        new_idx_ref, new_k_ref, new_v_ref = refs[:3]
        refs = refs[3:]
    else:
        old = refs[:3]
        refs = refs[3:]
    arrays = refs[: len(counts)]
    refs = refs[len(counts) :]
    if last:
        out_ref = refs[0]
        acc, m, l, buf, sem = refs[1:]
    else:
        acc, m, l = refs[:3]
        buf, sem = refs[3:]

    total = sum(min(c, CAP) for c in counts)
    at = 0
    plan = []
    for array, count in zip(arrays, counts):
        for k in range(CAP):
            plan.append((at, array, k, count > CAP))
            at += 1
    for at, array, k, dynamic in plan:

        @pl.when(table_ref[2 * at] >= 0)
        def _(at=at, array=array, k=k, dynamic=dynamic):
            where = table_ref[2 * at + 1] if dynamic else k
            pltpu.make_async_copy(array.at[where], buf.at[at], sem.at[at]).start()

    def tile_queries(tile):
        rows = pl.ds(pl.multiple_of(tile * SUB, SUB), SUB)
        return jnp.concatenate(
            [q_ref[rows, h * HD : (h + 1) * HD] for h in range(GROUP)], axis=0
        )

    def scores(tile, keys, idx):
        s = lax.dot_general(
            tile_queries(tile), keys, (((1,), (1,)), ((), ())), preferred_element_type=jnp.float32
        )
        return jnp.where(idx <= pos_ref[tile], s, -1e30)

    if first:

        def start(tile, carry):
            s = scores(tile, new_k_ref[...], new_idx_ref[...])
            top = jnp.max(s, axis=1, keepdims=True)
            p = jnp.exp2((s - top) * EXP2)
            m[tile] = top
            l[tile] = jnp.sum(p, axis=1, keepdims=True)
            acc[tile] = jnp.dot(
                p.astype(jnp.bfloat16), new_v_ref[...], preferred_element_type=jnp.float32
            )
            return carry

        lax.fori_loop(0, TILES, start, 0)
    else:
        for new, prev in zip((acc, m, l), old):
            new[...] = prev[...]

    def item(at, carry):
        j = table_ref[2 * at]

        @pl.when(j >= 0)
        def _():
            pltpu.make_async_copy(arrays[0].at[0], buf.at[at], sem.at[at]).wait()

            def step(tile, carry):
                s = scores(tile, buf[at, 0], idx_ref[j])
                before = m[tile]
                top = jnp.maximum(before, jnp.max(s, axis=1, keepdims=True))
                p = jnp.exp2((s - top) * EXP2)
                fade = jnp.exp2((before - top) * EXP2)
                m[tile] = top
                l[tile] = l[tile] * fade + jnp.sum(p, axis=1, keepdims=True)
                acc[tile] = acc[tile] * fade + jnp.dot(
                    p.astype(jnp.bfloat16), buf[at, 1], preferred_element_type=jnp.float32
                )
                return carry

            lax.fori_loop(j // 2, TILES, step, 0)

        return carry

    lax.fori_loop(0, total, item, 0)

    if last:
        for tile in range(TILES):
            done = (acc[tile] / l[tile]).astype(jnp.bfloat16)
            for h in range(GROUP):
                out_ref[tile * SUB : (tile + 1) * SUB, h * HD : (h + 1) * HD] = done[
                    h * SUB : (h + 1) * SUB
                ]


def attend(table, query, pos, idx, extra, arrays, first, last):
    counts = [a.shape[0] for a in arrays]
    cands = CAP * len(arrays)
    state = [
        jax.ShapeDtypeStruct((TILES, ROWS, HD), jnp.float32),
        jax.ShapeDtypeStruct((TILES, ROWS, 1), jnp.float32),
        jax.ShapeDtypeStruct((TILES, ROWS, 1), jnp.float32),
    ]
    scratch = [
        pltpu.VMEM((cands, 2, DOC, HD), jnp.bfloat16),
        pltpu.SemaphoreType.DMA((cands,)),
    ]
    if last:
        out_shape = jax.ShapeDtypeStruct((TOKENS, GROUP * HD), jnp.bfloat16)
        scratch = [pltpu.VMEM(s.shape, s.dtype) for s in state] + scratch
        out_specs = VMEM
    else:
        out_shape, out_specs = state, [VMEM] * 3
    return pl.pallas_call(
        functools.partial(attend_kernel, counts, first, last),
        out_shape=out_shape,
        in_specs=[SMEM, VMEM, VMEM, VMEM] + [VMEM] * 3 + [ANY] * len(arrays),
        out_specs=out_specs,
        scratch_shapes=scratch,
        compiler_params=pltpu.CompilerParams(vmem_limit_bytes=40 << 20),
        cost_estimate=pl.CostEstimate(
            flops=2 * 2 * 1280 * 512 * 128 * len(arrays) // 2,
            bytes_accessed=(6 << 20) + len(arrays) * (1 << 18),
            transcendentals=1280 * 512 * len(arrays) // 2,
        ),
        name="attend",
    )(table, query, pos, idx, *extra, *arrays)


def project_kernel(place_ref, *refs):
    parts, w_ref, out_ref = refs[:-2], refs[-2], refs[-1]
    total = None
    for n, part in enumerate(parts):
        rows = pl.ds(pl.multiple_of(place_ref[n] * (GROUP * HD), GROUP * HD), GROUP * HD)
        term = jnp.dot(part[...], w_ref[rows, :], preferred_element_type=jnp.float32)
        total = term if total is None else total + term
    out_ref[...] = total.astype(jnp.bfloat16)


def project(place, parts, w_out):
    return pl.pallas_call(
        project_kernel,
        out_shape=jax.ShapeDtypeStruct((TOKENS, w_out.shape[1]), jnp.bfloat16),
        in_specs=[SMEM] + [VMEM] * (len(parts) + 1),
        out_specs=VMEM,
        compiler_params=pltpu.CompilerParams(vmem_limit_bytes=40 << 20),
        cost_estimate=pl.CostEstimate(
            flops=2 * TOKENS * 4096 * 512, bytes_accessed=7 << 20, transcendentals=0
        ),
        name="project",
    )(place, *parts, w_out)


def ring(block, by):
    return lax.ppermute(block, "tp", [(i, (i + 2 * by) % KVH) for i in range(KVH)])


def other_core(block):
    return lax.ppermute(block, "tp", [(i, i ^ 1) for i in range(KVH)])


def gather(own):
    half = TOKENS // 2
    up, down = ring(own, 1), ring(own, -1)
    far_up, far_down = ring(up[:half], 1), ring(down[half:], -1)
    far = jnp.concatenate([far_up, far_down], axis=0)
    parts = [own, up, down, far]
    return parts + [other_core(p) for p in parts]


def body(
    sel_hidden,
    norm_gain,
    w_query,
    w_key,
    w_value,
    w_out,
    doc_cache,
    home,
    doc_ids,
    doc_len,
    positions,
):
    me = lax.axis_index("grp")
    stored = doc_cache.shape[0]
    served = sel_hidden.shape[0]
    per_group = served * RETRIEVED

    with jax.named_scope("tables"):
        location = home[doc_ids].reshape(GROUPS, per_group)
        owner = location // stored
        slot_index = location % stored
        slots = jnp.arange(per_group, dtype=jnp.int32)
        earlier = (owner[:, :, None] == owner[:, None, :]) & (
            slots[None, None, :] < slots[None, :, None]
        )
        rank = jnp.sum(earlier.astype(jnp.int32), axis=2)
        ranks = jnp.arange(CAP, dtype=jnp.int32)
        match = (owner == me)[:, :, None] & (rank[:, :, None] == ranks)
        chosen = jnp.max(jnp.where(match, slot_index[:, :, None], -1), axis=1).reshape(-1)
    with jax.named_scope("pack"):
        packed = dict(zip(SHIFTS, pack(me.reshape(1), chosen, doc_cache)))
    with jax.named_scope("documents"):
        arrived = {}
        relayed = {s: shift(packed[KNIGHT[s]], s) for s in NEAR}
        for s in NEAR + DIAGONAL:
            arrived[s] = shift(packed[s], s)
        later = TWO + OPPOSITE
        held, _ = lax.optimization_barrier(
            (
                (relayed, {s: packed[s] for s in later}),
                [arrived[s] for s in NEAR + DIAGONAL],
            )
        )
        for s in later:
            arrived[s] = shift(held[1][s], s)
        for s in NEAR:
            arrived[KNIGHT[s]] = shift(held[0][s], (2, 0) if s[0] == 0 else (0, 2))

    with jax.named_scope("receive_tables"):
        x, y = me // SIDE, me % SIDE
        own_owner, own_rank, own_slot = owner[me], rank[me], slot_index[me]

        def table(r, shifts):
            rows = []
            span = slice(r * RETRIEVED, (r + 1) * RETRIEVED)
            sources = jnp.stack(
                [(x - dx) % SIDE * SIDE + (y - dy) % SIDE for dx, dy in shifts]
            )
            hit = (own_owner[span][None, None, :] == sources[:, None, None]) & (
                own_rank[span][None, None, :] == ranks[None, :, None]
            )
            j = jnp.max(
                jnp.where(hit, jnp.arange(RETRIEVED, dtype=jnp.int32), -1), axis=2
            )
            at = jnp.max(jnp.where(hit, own_slot[span][None, None, :], -1), axis=2)
            return jnp.stack([j, at], axis=-1).reshape(-1)

        doc_rows = (
            jnp.arange(RETRIEVED, dtype=jnp.int32)[:, None] * DOC
            + jnp.arange(DOC, dtype=jnp.int32)[None, :]
        )
        per_doc = positions.reshape(served, RETRIEVED, TOKENS // RETRIEVED)
        replaced = jnp.any(per_doc[:, :, :, None] == doc_rows[None, :, None, :], axis=2)
        lengths = doc_len[doc_ids.reshape(GROUPS, served, RETRIEVED)[me]]
        valid = jnp.arange(DOC, dtype=jnp.int32)[None, None, :] < lengths[:, :, None]
        key_index = jnp.where(valid & jnp.logical_not(replaced), doc_rows[None], FAR)[:, :, None, :]
        new_index = jnp.pad(positions, ((0, 0), (0, PADDED - TOKENS)), constant_values=FAR)
        row_pos = jnp.broadcast_to(
            positions.reshape(served, TILES, 1, SUB), (served, TILES, GROUP, SUB)
        ).reshape(served, TILES, ROWS, 1)

    with jax.named_scope("projections"):
        xf = sel_hidden.astype(jnp.float32)
        normed = (
            xf * lax.rsqrt(jnp.mean(xf * xf, axis=-1, keepdims=True) + 1e-05) * norm_gain
        ).astype(jnp.bfloat16)
        normed_rows = normed.reshape(served * TOKENS, normed.shape[2])

        def dot(w):
            out = jnp.dot(normed_rows, w, preferred_element_type=jnp.float32)
            return out.astype(jnp.bfloat16).reshape(served, TOKENS, w.shape[1])

        query, key_new, value_new = dot(w_query), dot(w_key), dot(w_value)
        pad = ((0, 0), (0, PADDED - TOKENS), (0, 0))
        key_new, value_new = jnp.pad(key_new, pad), jnp.pad(value_new, pad)

    with jax.named_scope("attention"):
        stages = [
            [(0, 0)] + NEAR + DIAGONAL,
            TWO + OPPOSITE + [KNIGHT[s] for s in NEAR],
        ]
        arrived[(0, 0)] = doc_cache
        outs = []
        for r in range(served):
            extra = [new_index[r : r + 1], key_new[r], value_new[r]]
            for n, shifts in enumerate(stages):
                extra = attend(
                    table(r, shifts),
                    query[r],
                    row_pos[r],
                    key_index[r],
                    extra,
                    [arrived[s] for s in shifts],
                    n == 0,
                    n == len(stages) - 1,
                )
            outs.append(extra)

    with jax.named_scope("output"):
        tp = lax.axis_index("tp")
        z, core = tp // 2, tp % 2
        planes = jnp.stack([z, (z + 3) % SIDE, (z + 1) % SIDE, (z + 2) % SIDE])
        place = jnp.concatenate([planes * 2 + core, planes * 2 + 1 - core]).astype(jnp.int32)
        mixed = [project(place, gather(o), w_out) for o in outs]
        return jnp.stack(mixed)


def solution(mesh):
    return jax.shard_map(
        body,
        mesh=mesh,
        in_specs=(
            P("grp", None, None),
            P(),
            P(None, "tp"),
            P(None, "tp"),
            P(None, "tp"),
            P(None, "tp"),
            P("grp", None, None, "tp"),
            P(),
            P(),
            P(),
            P("grp", None),
        ),
        out_specs=P("grp", None, "tp"),
        check_vma=False,
    )
```

```python
import functools
import math

import jax
import jax.numpy as jnp
from jax import lax
from jax.experimental import pallas as pl
from jax.experimental.pallas import tpu as pltpu
from jax.sharding import PartitionSpec as P

H = 32
KVH = 8
HD = 128
CAP = 2
GROUP = H // KVH
SIDE = 4
GROUPS = 16
STORED = 16
SLOTS = 16
PICK = 40
DOC = 512
TOKENS = 320
RETRIEVED = 8
TILES = 2
SUB = TOKENS // TILES
ROWS = SUB * GROUP
PADDED = 384
FAR = 2**30
EXP2 = HD ** (-0.5) * math.log2(math.e)

NEAR = [(1, 0), (3, 0), (0, 1), (0, 3)]
DIAGONAL = [(1, 1), (3, 3), (1, 3), (3, 1)]
OPPOSITE = [(2, 2)]
KNIGHT = [(1, 2), (3, 2), (2, 1), (2, 3)]
TWO = [(2, 0), (0, 2)]
CARRIED = {(2, 0): [(2, 0), (2, 1), (2, 3)], (0, 2): [(0, 2), (1, 2), (3, 2)]}
BLOCKS = [CARRIED[s] for s in TWO] + [[s] for s in DIAGONAL + NEAR + OPPOSITE]
STAGES = [[(0, 0)], TWO, DIAGONAL, NEAR, KNIGHT + OPPOSITE]
ROOM = 24 << 20

ANY = pl.BlockSpec(memory_space=pl.ANY)
HBM = pl.BlockSpec(memory_space=pltpu.HBM)
VMEM = pl.BlockSpec(memory_space=pltpu.VMEM)
SMEM = pl.BlockSpec(memory_space=pltpu.SMEM)


def shift(block, by):
    pairs = [
        (x * SIDE + y, (x + by[0]) % SIDE * SIDE + (y + by[1]) % SIDE)
        for x in range(SIDE)
        for y in range(SIDE)
    ]
    return lax.ppermute(block, "grp", pairs)


def pack_kernel(me_ref, home_ref, ids_ref, len_ref, cache_ref, *refs):
    out_refs, refs = refs[: len(BLOCKS)], refs[len(BLOCKS) :]
    table_ref, chosen, sem = refs
    me = me_ref[0]
    x, y = me // SIDE, me % SIDE

    def locate(g, i):
        return home_ref[ids_ref[g * 2 + i // RETRIEVED, i % RETRIEVED]]

    def outgoing(g, carry):
        one, two = jnp.int32(-1), jnp.int32(-1)
        for i in range(SLOTS):
            slot = locate(g, i) - me * STORED
            hit = (slot >= 0) & (slot < STORED)
            two = jnp.where(hit, one, two)
            one = jnp.where(hit, slot, one)
        chosen[g * CAP] = jnp.where(two >= 0, two, one)
        chosen[g * CAP + 1] = jnp.where(two >= 0, one, -1)
        return carry

    lax.fori_loop(0, GROUPS, outgoing, 0)

    def each(act):
        at = 0
        for block, out in zip(BLOCKS, out_refs):
            for n, (dx, dy) in enumerate(block):
                g = (x + dx) % SIDE * SIDE + (y + dy) % SIDE
                for k in range(CAP):
                    doc = chosen[g * CAP + k]

                    @pl.when(doc >= 0)
                    def _(at=at, doc=doc, out=out.at[n * CAP + k]):
                        act(at, doc, out)

                    at += 1

    def read(at, doc, out):
        return pltpu.make_async_copy(cache_ref.at[doc], out, sem.at[at])

    each(lambda at, doc, out: read(at, doc, out).start())

    for at in range(GROUPS * CAP):
        table_ref[at] = jnp.int32(-1)
    for i in range(SLOTS):
        doc = ids_ref[me * 2 + i // RETRIEVED, i % RETRIEVED]
        location = home_ref[doc]
        at = location // STORED * CAP
        table_ref[at + jnp.where(table_ref[at] >= 0, 1, 0)] = jnp.int32(i)
        table_ref[GROUPS * CAP + i] = location % STORED
        table_ref[GROUPS * CAP + SLOTS + i] = len_ref[doc]

    each(lambda at, doc, out: read(at, doc, out).wait())


def pack(me, home, ids, lengths, cache):
    shapes = [(CAP * len(b), 2, DOC, HD) for b in BLOCKS]
    total = sum(s[0] for s in shapes)
    *packed, table = pl.pallas_call(
        pack_kernel,
        out_shape=[jax.ShapeDtypeStruct(s, jnp.bfloat16) for s in shapes]
        + [jax.ShapeDtypeStruct((GROUPS * CAP + 2 * SLOTS,), jnp.int32)],
        in_specs=[SMEM] * 4 + [HBM],
        out_specs=[VMEM] * len(BLOCKS) + [SMEM],
        scratch_shapes=[
            pltpu.SMEM((GROUPS * CAP,), jnp.int32),
            pltpu.SemaphoreType.DMA((total,)),
        ],
        compiler_params=pltpu.CompilerParams(vmem_limit_bytes=ROOM),
        cost_estimate=pl.CostEstimate(flops=0, bytes_accessed=10 << 20, transcendentals=0),
        name="pack",
    )(me, home, ids, lengths, cache)
    return packed, table


def attend_kernel(shifts, base, count, first, last, *refs):
    refs = list(refs)
    me_ref, table_ref, q_ref, pos_ref = refs[:4]
    if first:
        new_idx_ref, new_k_ref, new_v_ref = refs[4:7]
    arrays, refs = refs[7 : 7 + len(shifts)], refs[7 + len(shifts) :]
    acc, top_ref, sum_ref, *refs = refs
    if last:
        out_ref, *refs = refs
    buf, items, sem = refs
    me = me_ref[0]
    x, y = me // SIDE, me % SIDE

    found = jnp.int32(0)
    for (dx, dy), array in zip(shifts, arrays):
        source = (x - dx + SIDE) % SIDE * SIDE + (y - dy + SIDE) % SIDE
        for k in range(CAP):
            i = table_ref[source * CAP + k]
            mine = (i >= base * RETRIEVED) & (i < (base + count) * RETRIEVED)

            @pl.when(mine)
            def _(i=i, array=array, k=k, at=found, own=(dx, dy) == (0, 0)):
                where = table_ref[GROUPS * CAP + i] if own else k
                items[at] = i
                pltpu.make_async_copy(array.at[where], buf.at[at], sem.at[at]).start()

            found = found + jnp.where(mine, 1, 0)

    def scores(r, tile, keys, idx):
        rows = pl.ds(pl.multiple_of(tile * SUB, SUB), SUB)
        q = jnp.concatenate(
            [q_ref[r, rows, h * HD : (h + 1) * HD] for h in range(GROUP)], axis=0
        )
        s = lax.dot_general(
            q, keys, (((1,), (1,)), ((), ())), preferred_element_type=jnp.float32
        )
        return jnp.where(idx <= pos_ref[r, tile], s, -1e30)

    def weigh(s, top):
        p = jnp.exp2((s - jnp.concatenate([top] * (s.shape[1] // HD), axis=1)) * EXP2)
        parts = [p[:, c : c + HD] for c in range(0, s.shape[1], HD)]
        return p.astype(jnp.bfloat16), functools.reduce(jnp.add, parts)

    if first:

        def start(at, carry):
            r, tile = at // TILES, at % TILES
            s = scores(r, tile, new_k_ref[r], new_idx_ref[r])
            top = jnp.broadcast_to(jnp.max(s, axis=1, keepdims=True), (ROWS, HD))
            p, sums = weigh(s, top)
            top_ref[r, tile] = top
            sum_ref[r, tile] = sums
            acc[r, tile] = jnp.dot(p, new_v_ref[r], preferred_element_type=jnp.float32)
            return carry

        lax.fori_loop(0, count * TILES, start, 0)

    def item(at, carry):
        i = items[at]
        r, j = i // RETRIEVED, i % RETRIEVED
        length = table_ref[GROUPS * CAP + SLOTS + i]
        row = lax.broadcasted_iota(jnp.int32, (1, DOC), 1)
        idx = row + j * DOC
        per = RETRIEVED // TILES
        picked = pos_ref[r, j // per, pl.ds(pl.multiple_of(j % per * PICK, PICK), PICK)]
        replaced = jnp.max(jnp.where(picked == idx, 1, 0), axis=0, keepdims=True)
        idx = jnp.where((row < length) & (replaced == 0), idx, FAR)
        pltpu.make_async_copy(arrays[0].at[0], buf.at[at], sem.at[at]).wait()

        def step(tile, carry):
            s = scores(r, tile, buf[at, 0], idx)
            before = top_ref[r, tile]
            top = jnp.maximum(before, jnp.max(s, axis=1, keepdims=True))
            fade = jnp.exp2((before - top) * EXP2)
            p, sums = weigh(s, top)
            top_ref[r, tile] = top
            sum_ref[r, tile] = sum_ref[r, tile] * fade + sums
            acc[r, tile] = acc[r, tile] * fade + jnp.dot(
                p, buf[at, 1], preferred_element_type=jnp.float32
            )
            return carry

        lax.fori_loop(j // per, TILES, step, 0)
        return carry

    lax.fori_loop(0, found, item, 0)

    if last:
        for tile in range(TILES):
            sums = jnp.sum(sum_ref[base, tile], axis=1, keepdims=True)
            done = (acc[base, tile] / sums).astype(jnp.bfloat16)
            for h in range(GROUP):
                out_ref[tile * SUB : (tile + 1) * SUB, h * HD : (h + 1) * HD] = done[
                    h * SUB : (h + 1) * SUB
                ]


def attend(me, table, query, pos, extra, arrays, shifts, base, count, first, last):
    cands = CAP * len(arrays)

    state = jax.ShapeDtypeStruct((query.shape[0], TILES, ROWS, HD), jnp.float32)
    out_shape = [state] * 3
    if last:
        out_shape.append(jax.ShapeDtypeStruct((TOKENS, GROUP * HD), jnp.bfloat16))
    return pl.pallas_call(
        functools.partial(attend_kernel, shifts, base, count, first, last),
        out_shape=out_shape,
        in_specs=[SMEM, SMEM] + [VMEM] * 5 + [ANY] * len(arrays),
        out_specs=[VMEM] * len(out_shape),
        scratch_shapes=[
            pltpu.VMEM((cands, 2, DOC, HD), jnp.bfloat16),
            pltpu.SMEM((cands,), jnp.int32),
            pltpu.SemaphoreType.DMA((cands,)),
        ],
        input_output_aliases={} if first else {4: 0, 5: 1, 6: 2},
        compiler_params=pltpu.CompilerParams(vmem_limit_bytes=ROOM),
        cost_estimate=pl.CostEstimate(
            flops=count * 2 * 1280 * 512 * 128 * len(arrays),
            bytes_accessed=count * ((4 << 20) + len(arrays) * (1 << 17)),
            transcendentals=count * 1280 * 512 * len(arrays) // 2,
        ),
        name="attend",
    )(me, table, query, pos, *extra, *arrays)


def project_kernel(spans, r, place_ref, w_ref, *refs):
    parts, (out_ref, done, sem) = refs[: len(spans)], refs[-3:]
    width, half = GROUP * HD, TOKENS // 2
    total = {}
    for part, (n, lo, hi) in zip(parts, spans):
        rows = pl.ds(pl.multiple_of(place_ref[n] * width, width), width)
        term = jnp.dot(part[...], w_ref[rows, :], preferred_element_type=jnp.float32)
        for at in range(lo, hi, half):
            piece = term[at - lo : at - lo + half]
            total[at] = total[at] + piece if at in total else piece
    for at, value in total.items():
        done[at : at + half] = value.astype(jnp.bfloat16)
    copy = pltpu.make_async_copy(done, out_ref.at[r], sem)
    copy.start()
    copy.wait()


def project(place, r, served, pieces, w_out, before):
    parts = [p for _, _, _, p in pieces]
    spans = [(n, lo, hi) for n, lo, hi, _ in pieces]
    more = [] if before is None else [before]
    return pl.pallas_call(
        functools.partial(project_kernel, spans, r),
        out_shape=jax.ShapeDtypeStruct((served, TOKENS, w_out.shape[1]), jnp.bfloat16),
        in_specs=[SMEM] + [VMEM] * (len(parts) + 1) + [HBM] * len(more),
        out_specs=HBM,
        scratch_shapes=[
            pltpu.VMEM((TOKENS, w_out.shape[1]), jnp.bfloat16),
            pltpu.SemaphoreType.DMA,
        ],
        input_output_aliases={len(parts) + 2: 0} if more else {},
        compiler_params=pltpu.CompilerParams(vmem_limit_bytes=ROOM),
        cost_estimate=pl.CostEstimate(
            flops=2 * TOKENS * 4096 * 512, bytes_accessed=7 << 20, transcendentals=0
        ),
        name="project",
    )(place, w_out, *parts, *more)


def ring(block, by):
    return lax.ppermute(block, "tp", [(i, (i + 2 * by) % KVH) for i in range(KVH)])


def other_core(block):
    return lax.ppermute(block, "tp", [(i, i ^ 1) for i in range(KVH)])


def gather(own):
    half = TOKENS // 2
    up, down = ring(own, 1), ring(own, -1)
    far_up, far_down = ring(up[:half], 1), ring(down[half:], -1)
    same = [(0, 0, TOKENS, own), (1, 0, TOKENS, up), (2, 0, TOKENS, down)]
    same += [(3, 0, half, far_up), (3, half, TOKENS, far_down)]
    return same + [(n + SIDE, lo, hi, other_core(p)) for n, lo, hi, p in same]


def body(
    sel_hidden,
    norm_gain,
    w_query,
    w_key,
    w_value,
    w_out,
    doc_cache,
    home,
    doc_ids,
    doc_len,
    positions,
):
    me = lax.axis_index("grp").astype(jnp.int32).reshape(1)
    served = sel_hidden.shape[0]

    with jax.named_scope("pack"):
        packed, table = pack(me, home, doc_ids, doc_len, doc_cache)
        packed = dict(zip([b[0] for b in BLOCKS], packed))

    with jax.named_scope("positions"):
        new_index = jnp.pad(
            positions, ((0, 0), (0, PADDED - TOKENS)), constant_values=FAR
        ).reshape(served, 1, PADDED)
        row_pos = jnp.broadcast_to(
            positions.reshape(served, TILES, 1, SUB), (served, TILES, GROUP, SUB)
        ).reshape(served, TILES, ROWS, 1)

    with jax.named_scope("projections"):
        xf = sel_hidden.astype(jnp.float32)
        normed = (
            xf * lax.rsqrt(jnp.mean(xf * xf, axis=-1, keepdims=True) + 1e-05) * norm_gain
        ).astype(jnp.bfloat16)
        normed_rows = normed.reshape(served * TOKENS, normed.shape[2])

        def dot(w):
            out = jnp.dot(normed_rows, w, preferred_element_type=jnp.float32)
            return out.astype(jnp.bfloat16).reshape(served, TOKENS, w.shape[1])

        query, key_new, value_new = dot(w_query), dot(w_key), dot(w_value)
        pad = ((0, 0), (0, PADDED - TOKENS), (0, 0))
        key_new, value_new = jnp.pad(key_new, pad), jnp.pad(value_new, pad)

    arrived = {(0, 0): doc_cache}

    def after(blocks, *done):
        return lax.optimization_barrier((blocks, done))[0]

    def send(names, blocks, hops):
        with jax.named_scope("documents"):
            for s, block, hop in zip(names, blocks, hops):
                arrived[s] = shift(block, hop)

    def attention(n, state, base, count):
        shifts, last = STAGES[n], n == len(STAGES) - 1
        with jax.named_scope("attention"):
            return attend(
                me,
                table,
                query,
                row_pos,
                state,
                [arrived[s] for s in shifts],
                shifts,
                base,
                count,
                n == 0,
                last,
            )

    send(TWO, [packed[s] for s in TWO], TWO)
    send(DIAGONAL, [packed[s] for s in DIAGONAL], DIAGONAL)
    state = attention(0, [new_index, key_new, value_new], 0, served)
    blocks = after([packed[s] for s in NEAR], [arrived[s] for s in TWO], state)
    send(NEAR, blocks, NEAR)
    state = attention(1, state, 0, served)
    blocks = []
    for s in KNIGHT:
        through = (0, 2) if s[1] == 2 else (2, 0)
        at = CAP * CARRIED[through].index(s)
        blocks.append(arrived[through][at : at + CAP])
    blocks = after(blocks, [arrived[s] for s in DIAGONAL], state)
    send(KNIGHT, blocks, NEAR)
    state = attention(2, state, 0, served)
    blocks = after([packed[s] for s in OPPOSITE], [arrived[s] for s in NEAR], state)
    send(OPPOSITE, blocks, OPPOSITE)
    state = attention(3, state, 0, served)
    outs = []
    for r in range(served):
        *state, out = attention(4, state, r, 1)
        outs.append(out)

    with jax.named_scope("output"):
        tp = lax.axis_index("tp")
        z, core = tp // 2, tp % 2
        planes = jnp.stack([z, (z + 3) % SIDE, (z + 1) % SIDE, (z + 2) % SIDE])
        place = jnp.concatenate([planes * 2 + core, planes * 2 + 1 - core]).astype(jnp.int32)
        gathered = [gather(o) for o in outs]
        mixed = None
        for r in range(served):
            mixed = project(place, r, served, gathered[r], w_out, mixed)
        return mixed


def solution(mesh):
    return jax.shard_map(
        body,
        mesh=mesh,
        in_specs=(
            P("grp", None, None),
            P(),
            P(None, "tp"),
            P(None, "tp"),
            P(None, "tp"),
            P(None, "tp"),
            P("grp", None, None, "tp"),
            P(),
            P(),
            P(),
            P("grp", None),
        ),
        out_specs=P("grp", None, "tp"),
        check_vma=False,
    )
```

```python
import functools
import math

import jax
import jax.numpy as jnp
from jax import lax
from jax.experimental import pallas as pl
from jax.experimental.pallas import tpu as pltpu
from jax.sharding import PartitionSpec as P

H = 32
KVH = 8
HD = 128
CAP = 2
GROUP = H // KVH
SIDE = 4
GROUPS = 16
STORED = 16
SLOTS = 16
PICK = 40
DOC = 512
TOKENS = 320
RETRIEVED = 8
TILES = 4
SUB = TOKENS // TILES
ROWS = SUB * GROUP
PADDED = 384
FAR = 2**30
EXP2 = HD ** (-0.5) * math.log2(math.e)

NEAR = [(1, 0), (3, 0), (0, 1), (0, 3)]
DIAGONAL = [(1, 1), (3, 3), (1, 3), (3, 1)]
OPPOSITE = [(2, 2)]
KNIGHT = [(1, 2), (3, 2), (2, 1), (2, 3)]
TWO = [(2, 0), (0, 2)]
CARRIED = {(2, 0): [(2, 0), (2, 1), (2, 3)], (0, 2): [(0, 2), (1, 2), (3, 2)]}
EARLY = [CARRIED[s] for s in TWO]
LATE = [[s] for s in DIAGONAL + NEAR + OPPOSITE]
CHOSEN = GROUPS * CAP + 2 * SLOTS
STAGES = [[(0, 0)], TWO, DIAGONAL, NEAR + OPPOSITE, KNIGHT]
JOINED = []
ROOM = 24 << 20
ALL_ROOM = 56 << 20
PROJECT_ROOM = 56 << 20

ANY = pl.BlockSpec(memory_space=pl.ANY)
HBM = pl.BlockSpec(memory_space=pltpu.HBM)
VMEM = pl.BlockSpec(memory_space=pltpu.VMEM)
SMEM = pl.BlockSpec(memory_space=pltpu.SMEM)


def shift(block, by):
    pairs = [
        (x * SIDE + y, (x + by[0]) % SIDE * SIDE + (y + by[1]) % SIDE)
        for x in range(SIDE)
        for y in range(SIDE)
    ]
    return lax.ppermute(block, "grp", pairs)


def copy_chosen(table_ref, cache_ref, blocks, out_refs, stage, read_sem, write_sem, between):
    me = table_ref[CHOSEN + GROUPS * CAP]
    x, y = me // SIDE, me % SIDE

    def each(act):
        at = 0
        for block, out in zip(blocks, out_refs):
            for n, (dx, dy) in enumerate(block):
                g = (x + dx) % SIDE * SIDE + (y + dy) % SIDE
                for k in range(CAP):
                    doc = table_ref[CHOSEN + g * CAP + k]

                    @pl.when(doc >= 0)
                    def _(at=at, doc=doc, out=out.at[n * CAP + k]):
                        act(at, doc, out)

                    at += 1

    def read(at, doc):
        return pltpu.make_async_copy(cache_ref.at[doc], stage.at[at], read_sem.at[at])

    def write(at, out):
        return pltpu.make_async_copy(stage.at[at], out, write_sem.at[at])

    def forward(at, doc, out):
        read(at, doc).wait()
        write(at, out).start()

    each(lambda at, doc, out: read(at, doc).start())
    between()
    each(forward)
    each(lambda at, doc, out: write(at, out).wait())


def first_pack_kernel(me_ref, home_ref, ids_ref, len_ref, cache_ref, *refs):
    out_refs, (table_ref, *scratch) = refs[: len(EARLY)], refs[len(EARLY) :]
    me = me_ref[0]

    def outgoing(g, carry):
        one, two = jnp.int32(-1), jnp.int32(-1)
        for i in range(SLOTS):
            slot = home_ref[ids_ref[g * SLOTS + i]] - me * STORED
            hit = (slot >= 0) & (slot < STORED)
            two = jnp.where(hit, one, two)
            one = jnp.where(hit, slot, one)
        table_ref[CHOSEN + g * CAP] = jnp.where(two >= 0, two, one)
        table_ref[CHOSEN + g * CAP + 1] = jnp.where(two >= 0, one, -1)
        return carry

    lax.fori_loop(0, GROUPS, outgoing, 0)
    table_ref[CHOSEN + GROUPS * CAP] = me

    def incoming():
        for at in range(GROUPS * CAP):
            table_ref[at] = jnp.int32(-1)
        for i in range(SLOTS):
            doc = ids_ref[me * SLOTS + i]
            location = home_ref[doc]
            at = location // STORED * CAP
            table_ref[at + jnp.where(table_ref[at] >= 0, 1, 0)] = jnp.int32(i)
            table_ref[GROUPS * CAP + i] = location % STORED
            table_ref[GROUPS * CAP + SLOTS + i] = len_ref[doc]

    copy_chosen(table_ref, cache_ref, EARLY, out_refs, *scratch, incoming)


def second_pack_kernel(table_ref, cache_ref, *refs):
    out_refs, scratch = refs[: len(LATE)], refs[len(LATE) :]
    copy_chosen(table_ref, cache_ref, LATE, out_refs, *scratch, lambda: None)


def pack(kernel, blocks, scalars, cache, with_table):
    shapes = [(CAP * len(b), 2, DOC, HD) for b in blocks]
    total = sum(s[0] for s in shapes)
    table = [jax.ShapeDtypeStruct((CHOSEN + GROUPS * CAP + 1,), jnp.int32)] if with_table else []
    return pl.pallas_call(
        kernel,
        out_shape=[jax.ShapeDtypeStruct(s, jnp.bfloat16) for s in shapes] + table,
        in_specs=[SMEM] * len(scalars) + [HBM],
        out_specs=[HBM] * len(blocks) + [SMEM] * len(table),
        scratch_shapes=[
            pltpu.VMEM((total, 2, DOC, HD), jnp.bfloat16),
            pltpu.SemaphoreType.DMA((total,)),
            pltpu.SemaphoreType.DMA((total,)),
        ],
        compiler_params=pltpu.CompilerParams(vmem_limit_bytes=ALL_ROOM),
        cost_estimate=pl.CostEstimate(flops=0, bytes_accessed=5 << 20, transcendentals=0),
        name="pack",
    )(*scalars, cache)


def attend_kernel(shifts, count, first, last, *refs):
    refs = list(refs)
    table_ref, q_ref, pos_ref = refs[:3]
    if first:
        new_idx_ref, new_k_ref, new_v_ref = refs[3:6]
    arrays, refs = refs[6 : 6 + len(shifts)], refs[6 + len(shifts) :]
    acc, top_ref, sum_ref, *refs = refs
    if last:
        out_ref, *refs = refs
    buf, items, sem = refs
    me = table_ref[CHOSEN + GROUPS * CAP]
    x, y = me // SIDE, me % SIDE

    found = jnp.int32(0)
    for (dx, dy), array in zip(shifts, arrays):
        skip = CAP if (dx, dy) in JOINED else 0
        source = (x - dx + SIDE) % SIDE * SIDE + (y - dy + SIDE) % SIDE
        for k in range(CAP):
            i = table_ref[source * CAP + k]
            mine = i >= 0

            @pl.when(mine)
            def _(i=i, array=array, k=k, at=found, own=(dx, dy) == (0, 0)):
                where = table_ref[GROUPS * CAP + i] if own else k + skip
                items[at] = i
                pltpu.make_async_copy(array.at[where], buf.at[at], sem.at[at]).start()

            found = found + jnp.where(mine, 1, 0)

    def scores(r, tile, wide, keys, idx):
        q = []
        for n in range(wide):
            rows = pl.ds(pl.multiple_of((tile + n) * SUB, SUB), SUB)
            q += [q_ref[r, rows, h * HD : (h + 1) * HD] for h in range(GROUP)]
        s = lax.dot_general(
            jnp.concatenate(q, axis=0),
            keys,
            (((1,), (1,)), ((), ())),
            preferred_element_type=jnp.float32,
        )
        pos = pos_ref[r, pl.ds(tile, wide)].reshape(wide * ROWS, 1)
        return jnp.where(idx <= pos, s, -1e30)

    def weigh(s, top):
        p = jnp.exp2((s - jnp.concatenate([top] * (s.shape[1] // HD), axis=1)) * EXP2)
        parts = [p[:, c : c + HD] for c in range(0, s.shape[1], HD)]
        return p.astype(jnp.bfloat16), functools.reduce(jnp.add, parts)

    def put(ref, r, tile, wide, value):
        ref[r, pl.ds(tile, wide)] = value.reshape(wide, ROWS, HD)

    if first:

        def start(at, carry):
            r, tile = at // (TILES // 2), at % (TILES // 2) * 2
            s = scores(r, tile, 2, new_k_ref[r], new_idx_ref[r])
            top = jnp.broadcast_to(jnp.max(s, axis=1, keepdims=True), (2 * ROWS, HD))
            p, sums = weigh(s, top)
            put(top_ref, r, tile, 2, top)
            put(sum_ref, r, tile, 2, sums)
            value = jnp.dot(p, new_v_ref[r], preferred_element_type=jnp.float32)
            put(acc, r, tile, 2, value)
            return carry

        lax.fori_loop(0, count * TILES // 2, start, 0)

    def item(at, carry):
        i = items[at]
        r, j = i // RETRIEVED, i % RETRIEVED
        length = table_ref[GROUPS * CAP + SLOTS + i]
        row = lax.broadcasted_iota(jnp.int32, (1, DOC), 1)
        idx = row + j * DOC
        per = RETRIEVED // TILES
        picked = pos_ref[r, j // per, pl.ds(pl.multiple_of(j % per * PICK, PICK), PICK)]
        replaced = jnp.max(jnp.where(picked == idx, 1, 0), axis=0, keepdims=True)
        idx = jnp.where((row < length) & (replaced == 0), idx, FAR)
        pltpu.make_async_copy(arrays[0].at[0], buf.at[at], sem.at[at]).wait()

        def step(tile, wide):
            def get(ref):
                return ref[r, pl.ds(tile, wide)].reshape(wide * ROWS, HD)

            s = scores(r, tile, wide, buf[at, 0], idx)
            before = get(top_ref)
            top = jnp.maximum(before, jnp.max(s, axis=1, keepdims=True))
            fade = jnp.exp2((before - top) * EXP2)
            p, sums = weigh(s, top)
            put(top_ref, r, tile, wide, top)
            put(sum_ref, r, tile, wide, get(sum_ref) * fade + sums)
            value = jnp.dot(p, buf[at, 1], preferred_element_type=jnp.float32)
            put(acc, r, tile, wide, get(acc) * fade + value)

        tile = j // per

        @pl.when(tile % 2 == 1)
        def _():
            step(tile, 1)

        def pair(n, carry):
            step(n * 2, 2)
            return carry

        lax.fori_loop((tile + 1) // 2, TILES // 2, pair, 0)
        return carry

    lax.fori_loop(0, found, item, 0)

    if last:
        for r in range(count):
            for tile in range(TILES):
                sums = jnp.sum(sum_ref[r, tile], axis=1, keepdims=True)
                done = (acc[r, tile] / sums).astype(jnp.bfloat16)
                rows = slice(r * TOKENS + tile * SUB, r * TOKENS + (tile + 1) * SUB)
                for h in range(GROUP):
                    out_ref[rows, h * HD : (h + 1) * HD] = done[h * SUB : (h + 1) * SUB]


def attend(table, query, pos, extra, arrays, shifts, first, last):
    cands, count = CAP * len(arrays), query.shape[0]

    state = jax.ShapeDtypeStruct((count, TILES, ROWS, HD), jnp.float32)
    out_shape = [state] * 3
    if last:
        out_shape.append(jax.ShapeDtypeStruct((count * TOKENS, GROUP * HD), jnp.bfloat16))
    return pl.pallas_call(
        functools.partial(attend_kernel, shifts, count, first, last),
        out_shape=out_shape,
        in_specs=[SMEM] + [VMEM] * 5 + [ANY] * len(arrays),
        out_specs=[VMEM] * len(out_shape),
        scratch_shapes=[
            pltpu.VMEM((cands, 2, DOC, HD), jnp.bfloat16),
            pltpu.SMEM((cands,), jnp.int32),
            pltpu.SemaphoreType.DMA((cands,)),
        ],
        input_output_aliases={} if first else {3: 0, 4: 1, 5: 2},
        compiler_params=pltpu.CompilerParams(vmem_limit_bytes=ROOM),
        cost_estimate=pl.CostEstimate(
            flops=count * 2 * 1280 * 512 * 128 * len(arrays),
            bytes_accessed=count * ((4 << 20) + len(arrays) * (1 << 17)),
            transcendentals=count * 1280 * 512 * len(arrays) // 2,
        ),
        name="attend",
    )(table, query, pos, *extra, *arrays)


def project_kernel(spans, last, place_ref, w_ref, *refs):
    parts, refs = refs[: len(spans)], refs[len(spans) :]
    if last:
        before_ref, *refs = refs
    out_ref, w, held, w_sem, part_sem = refs
    width = GROUP * HD
    order = list(dict.fromkeys(n for n, _, _ in spans))

    def weights(slot):
        rows = pl.ds(pl.multiple_of(place_ref[order[slot]] * width, width), width)
        return pltpu.make_async_copy(w_ref.at[rows], w.at[slot], w_sem.at[slot])

    def piece(at):
        n, lo, hi = spans[at]
        target = held.at[order.index(n), lo:hi]
        return pltpu.make_async_copy(parts[at], target, part_sem.at[at])

    for slot, n in enumerate(order):
        weights(slot).start()
        for at in range(len(spans)):
            if spans[at][0] == n:
                piece(at).start()
    total = before_ref[...] if last else None
    for slot, n in enumerate(order):
        weights(slot).wait()
        for at in range(len(spans)):
            if spans[at][0] == n:
                piece(at).wait()
        term = jnp.dot(held[slot], w[slot], preferred_element_type=jnp.float32)
        total = term if total is None else total + term
    out_ref[...] = total.astype(out_ref.dtype)


def project(place, pieces, w_out, before):
    spans, parts = [p[:3] for p in pieces], [p[3] for p in pieces]
    rows, columns = max(hi for _, _, hi in spans), w_out.shape[1]
    blocks, last = len({n for n, _, _ in spans}), before is not None
    return pl.pallas_call(
        functools.partial(project_kernel, spans, last),
        out_shape=jax.ShapeDtypeStruct((rows, columns), jnp.bfloat16 if last else jnp.float32),
        in_specs=[SMEM, HBM] + [ANY] * len(parts) + [VMEM] * last,
        out_specs=VMEM,
        scratch_shapes=[
            pltpu.VMEM((blocks, GROUP * HD, columns), jnp.bfloat16),
            pltpu.VMEM((blocks, rows, GROUP * HD), jnp.bfloat16),
            pltpu.SemaphoreType.DMA((blocks,)),
            pltpu.SemaphoreType.DMA((len(parts),)),
        ],
        compiler_params=pltpu.CompilerParams(vmem_limit_bytes=PROJECT_ROOM),
        cost_estimate=pl.CostEstimate(
            flops=2 * rows * blocks * 512 * 512, bytes_accessed=blocks << 20, transcendentals=0
        ),
        name="project",
    )(place, w_out, *parts, *([before] if last else []))


def ring(block, by):
    return lax.ppermute(block, "tp", [(i, (i + 2 * by) % KVH) for i in range(KVH)])


def other_core(block):
    return lax.ppermute(block, "tp", [(i, i ^ 1) for i in range(KVH)])


def body(
    sel_hidden,
    norm_gain,
    w_query,
    w_key,
    w_value,
    w_out,
    doc_cache,
    home,
    doc_ids,
    doc_len,
    positions,
):
    me = lax.axis_index("grp").astype(jnp.int32).reshape(1)
    served = sel_hidden.shape[0]

    with jax.named_scope("pack"):
        scalars = [me, home, doc_ids.reshape(-1), doc_len]
        *early, table = pack(first_pack_kernel, EARLY, scalars, doc_cache, True)
        late = list(pack(second_pack_kernel, LATE, [table], doc_cache, False))
        packed = {b[0]: p for b, p in zip(EARLY + LATE, early + late)}

    with jax.named_scope("positions"):
        new_index = jnp.pad(
            positions, ((0, 0), (0, PADDED - TOKENS)), constant_values=FAR
        ).reshape(served, 1, PADDED)
        row_pos = jnp.broadcast_to(
            positions.reshape(served, TILES, 1, SUB), (served, TILES, GROUP, SUB)
        ).reshape(served, TILES, ROWS, 1)

    with jax.named_scope("projections"):
        xf = sel_hidden.astype(jnp.float32)
        normed = (
            xf * lax.rsqrt(jnp.mean(xf * xf, axis=-1, keepdims=True) + 1e-05) * norm_gain
        ).astype(jnp.bfloat16)
        normed_rows = normed.reshape(served * TOKENS, normed.shape[2])

        def dot(w):
            out = jnp.dot(normed_rows, w, preferred_element_type=jnp.float32)
            return out.astype(jnp.bfloat16).reshape(served, TOKENS, w.shape[1])

        query, key_new, value_new = dot(w_query), dot(w_key), dot(w_value)
        pad = ((0, 0), (0, PADDED - TOKENS), (0, 0))
        key_new, value_new = jnp.pad(key_new, pad), jnp.pad(value_new, pad)

    arrived = {(0, 0): doc_cache}

    def after(blocks, *done):
        return lax.optimization_barrier((blocks, done))[0]

    def send(names, blocks, hops):
        with jax.named_scope("documents"):
            for s, block, hop in zip(names, blocks, hops):
                arrived[s] = shift(block, hop)

    def attention(n, state):
        shifts, last = STAGES[n], n == len(STAGES) - 1
        with jax.named_scope("attention"):
            return attend(
                table,
                query,
                row_pos,
                state,
                [arrived[s] for s in shifts],
                shifts,
                n == 0,
                last,
            )

    send(TWO, [packed[s] for s in TWO], TWO)
    send(DIAGONAL, [packed[s] for s in DIAGONAL], DIAGONAL)
    state = attention(0, [new_index, key_new, value_new])
    now = NEAR + OPPOSITE
    send(now, after([packed[s] for s in now], [arrived[s] for s in TWO], state), now)
    state = attention(1, state)
    blocks = []
    for s in KNIGHT:
        through = (0, 2) if s[1] == 2 else (2, 0)
        at = CAP * CARRIED[through].index(s)
        blocks.append(arrived[through][at : at + CAP])
    send(KNIGHT, after(blocks, [arrived[s] for s in DIAGONAL], state), NEAR)
    state = attention(2, state)
    state = attention(3, state)
    own = attention(len(STAGES) - 1, state)[-1]

    with jax.named_scope("output"):
        tp = lax.axis_index("tp")
        z, core = tp // 2, tp % 2
        planes = jnp.stack([z, (z + 3) % SIDE, (z + 1) % SIDE, (z + 2) % SIDE])
        place = jnp.concatenate([planes * 2 + core, planes * 2 + 1 - core]).astype(jnp.int32)
        rows = served * TOKENS
        half = rows // 2
        up, down, core = ring(own, 1), ring(own, -1), other_core(own)
        near = [(0, own), (4, core), (1, up), (2, down), (5, other_core(up)), (6, other_core(down))]
        near = [(n, 0, rows, p) for n, p in near]
        far = [ring(up[:half], 1), ring(down[half:], -1)]
        partial = project(place, near, w_out, None)
        far = lax.optimization_barrier((far, partial))[0]
        cross = [other_core(p) for p in far]
        pieces = [(3, 0, half, far[0]), (3, half, rows, far[1])]
        pieces += [(7, 0, half, cross[0]), (7, half, rows, cross[1])]
        mixed = project(place, pieces, w_out, partial)
        return mixed.reshape(served, TOKENS, w_out.shape[1])


def solution(mesh):
    return jax.shard_map(
        body,
        mesh=mesh,
        in_specs=(
            P("grp", None, None),
            P(),
            P(None, "tp"),
            P(None, "tp"),
            P(None, "tp"),
            P(None, "tp"),
            P("grp", None, None, "tp"),
            P(),
            P(),
            P(),
            P("grp", None),
        ),
        out_specs=P("grp", None, "tp"),
        check_vma=False,
    )
```

```python
import functools
import math

import jax
import jax.numpy as jnp
from jax import lax
from jax.experimental import pallas as pl
from jax.experimental.pallas import tpu as pltpu
from jax.sharding import PartitionSpec as P

H = 32
KVH = 8
HD = 128
CAP = 2
GROUP = H // KVH
SIDE = 4
GROUPS = 16
STORED = 16
SLOTS = 16
PICK = 40
DOC = 512
TOKENS = 320
RETRIEVED = 8
TILES = 4
SUB = TOKENS // TILES
ROWS = SUB * GROUP
PADDED = 384
FAR = 2**30
EXP2 = HD ** (-0.5) * math.log2(math.e)

NEAR = [(1, 0), (3, 0), (0, 1), (0, 3)]
DIAGONAL = [(1, 1), (3, 3), (1, 3), (3, 1)]
OPPOSITE = [(2, 2)]
KNIGHT = [(1, 2), (3, 2), (2, 1), (2, 3)]
TWO = [(2, 0), (0, 2)]
CARRIED = {(2, 0): [(2, 0), (2, 1), (2, 3)], (0, 2): [(0, 2), (1, 2), (3, 2)]}
EARLY = [CARRIED[s] for s in TWO]
LATE = [[s] for s in DIAGONAL + NEAR + OPPOSITE]
CHOSEN = GROUPS * CAP + 2 * SLOTS
STAGES = [[(0, 0)], TWO, DIAGONAL, NEAR + OPPOSITE, KNIGHT]
JOINED = []
ROOM = 24 << 20
ALL_ROOM = 56 << 20
PROJECT_ROOM = 24 << 20

ANY = pl.BlockSpec(memory_space=pl.ANY)
HBM = pl.BlockSpec(memory_space=pltpu.HBM)
VMEM = pl.BlockSpec(memory_space=pltpu.VMEM)
SMEM = pl.BlockSpec(memory_space=pltpu.SMEM)


def shift(block, by):
    pairs = [
        (x * SIDE + y, (x + by[0]) % SIDE * SIDE + (y + by[1]) % SIDE)
        for x in range(SIDE)
        for y in range(SIDE)
    ]
    return lax.ppermute(block, "grp", pairs)


def copy_chosen(table_ref, cache_ref, blocks, out_refs, stage, read_sem, write_sem, between):
    me = table_ref[CHOSEN + GROUPS * CAP]
    x, y = me // SIDE, me % SIDE

    def each(act):
        at = 0
        for block, out in zip(blocks, out_refs):
            for n, (dx, dy) in enumerate(block):
                g = (x + dx) % SIDE * SIDE + (y + dy) % SIDE
                for k in range(CAP):
                    doc = table_ref[CHOSEN + g * CAP + k]

                    @pl.when(doc >= 0)
                    def _(at=at, doc=doc, out=out.at[n * CAP + k]):
                        act(at, doc, out)

                    at += 1

    def read(at, doc):
        return pltpu.make_async_copy(cache_ref.at[doc], stage.at[at], read_sem.at[at])

    def write(at, out):
        return pltpu.make_async_copy(stage.at[at], out, write_sem.at[at])

    def forward(at, doc, out):
        read(at, doc).wait()
        write(at, out).start()

    each(lambda at, doc, out: read(at, doc).start())
    between()
    each(forward)
    each(lambda at, doc, out: write(at, out).wait())


def first_pack_kernel(me_ref, home_ref, ids_ref, len_ref, cache_ref, *refs):
    out_refs, (table_ref, *scratch) = refs[: len(EARLY)], refs[len(EARLY) :]
    me = me_ref[0]

    x, y = me // SIDE, me % SIDE

    def outgoing(g, carry):
        one, two = jnp.int32(-1), jnp.int32(-1)
        for i in range(SLOTS):
            slot = home_ref[ids_ref[g * SLOTS + i]] - me * STORED
            hit = (slot >= 0) & (slot < STORED)
            two = jnp.where(hit, one, two)
            one = jnp.where(hit, slot, one)
        table_ref[CHOSEN + g * CAP] = jnp.where(two >= 0, two, one)
        table_ref[CHOSEN + g * CAP + 1] = jnp.where(two >= 0, one, -1)
        return carry

    for block in EARLY:
        for dx, dy in block:
            outgoing((x + dx) % SIDE * SIDE + (y + dy) % SIDE, 0)
    table_ref[CHOSEN + GROUPS * CAP] = me

    def rest():
        lax.fori_loop(0, GROUPS, outgoing, 0)
        for at in range(GROUPS * CAP):
            table_ref[at] = jnp.int32(-1)
        for i in range(SLOTS):
            doc = ids_ref[me * SLOTS + i]
            location = home_ref[doc]
            at = location // STORED * CAP
            table_ref[at + jnp.where(table_ref[at] >= 0, 1, 0)] = jnp.int32(i)
            table_ref[GROUPS * CAP + i] = location % STORED
            table_ref[GROUPS * CAP + SLOTS + i] = len_ref[doc]

    copy_chosen(table_ref, cache_ref, EARLY, out_refs, *scratch, rest)


def second_pack_kernel(table_ref, cache_ref, *refs):
    out_refs, scratch = refs[: len(LATE)], refs[len(LATE) :]
    copy_chosen(table_ref, cache_ref, LATE, out_refs, *scratch, lambda: None)


def pack(kernel, blocks, scalars, cache, with_table):
    shapes = [(CAP * len(b), 2, DOC, HD) for b in blocks]
    total = sum(s[0] for s in shapes)
    table = [jax.ShapeDtypeStruct((CHOSEN + GROUPS * CAP + 1,), jnp.int32)] if with_table else []
    return pl.pallas_call(
        kernel,
        out_shape=[jax.ShapeDtypeStruct(s, jnp.bfloat16) for s in shapes] + table,
        in_specs=[SMEM] * len(scalars) + [HBM],
        out_specs=[HBM] * len(blocks) + [SMEM] * len(table),
        scratch_shapes=[
            pltpu.VMEM((total, 2, DOC, HD), jnp.bfloat16),
            pltpu.SemaphoreType.DMA((total,)),
            pltpu.SemaphoreType.DMA((total,)),
        ],
        compiler_params=pltpu.CompilerParams(vmem_limit_bytes=ALL_ROOM),
        cost_estimate=pl.CostEstimate(flops=0, bytes_accessed=5 << 20, transcendentals=0),
        name="pack",
    )(*scalars, cache)


def attend_kernel(shifts, count, first, last, *refs):
    refs = list(refs)
    table_ref, q_ref, pos_ref = refs[:3]
    if first:
        new_idx_ref, new_k_ref, new_v_ref = refs[3:6]
    arrays, refs = refs[6 : 6 + len(shifts)], refs[6 + len(shifts) :]
    acc, top_ref, sum_ref, *refs = refs
    if last:
        out_ref, *refs = refs
    buf, items, sem = refs
    me = table_ref[CHOSEN + GROUPS * CAP]
    x, y = me // SIDE, me % SIDE

    found = jnp.int32(0)
    for (dx, dy), array in zip(shifts, arrays):
        skip = CAP if (dx, dy) in JOINED else 0
        source = (x - dx + SIDE) % SIDE * SIDE + (y - dy + SIDE) % SIDE
        for k in range(CAP):
            i = table_ref[source * CAP + k]
            mine = i >= 0

            @pl.when(mine)
            def _(i=i, array=array, k=k, at=found, own=(dx, dy) == (0, 0)):
                where = table_ref[GROUPS * CAP + i] if own else k + skip
                items[at] = i
                pltpu.make_async_copy(array.at[where], buf.at[at], sem.at[at]).start()

            found = found + jnp.where(mine, 1, 0)

    def scores(r, tile, wide, keys, idx):
        q = []
        for n in range(wide):
            rows = pl.ds(pl.multiple_of((tile + n) * SUB, SUB), SUB)
            q += [q_ref[r, rows, h * HD : (h + 1) * HD] for h in range(GROUP)]
        s = lax.dot_general(
            jnp.concatenate(q, axis=0),
            keys,
            (((1,), (1,)), ((), ())),
            preferred_element_type=jnp.float32,
        )
        pos = pos_ref[r, pl.ds(tile, wide)].reshape(wide * ROWS, 1)
        return jnp.where(idx <= pos, s, -1e30)

    def weigh(s, top):
        p = jnp.exp2((s - jnp.concatenate([top] * (s.shape[1] // HD), axis=1)) * EXP2)
        parts = [p[:, c : c + HD] for c in range(0, s.shape[1], HD)]
        return p.astype(jnp.bfloat16), functools.reduce(jnp.add, parts)

    def put(ref, r, tile, wide, value):
        ref[r, pl.ds(tile, wide)] = value.reshape(wide, ROWS, HD)

    if first:

        def start(at, carry):
            r, tile = at // (TILES // 2), at % (TILES // 2) * 2
            s = scores(r, tile, 2, new_k_ref[r], new_idx_ref[r])
            top = jnp.broadcast_to(jnp.max(s, axis=1, keepdims=True), (2 * ROWS, HD))
            p, sums = weigh(s, top)
            put(top_ref, r, tile, 2, top)
            put(sum_ref, r, tile, 2, sums)
            value = jnp.dot(p, new_v_ref[r], preferred_element_type=jnp.float32)
            put(acc, r, tile, 2, value)
            return carry

        lax.fori_loop(0, count * TILES // 2, start, 0)

    def item(at, carry):
        i = items[at]
        r, j = i // RETRIEVED, i % RETRIEVED
        length = table_ref[GROUPS * CAP + SLOTS + i]
        row = lax.broadcasted_iota(jnp.int32, (1, DOC), 1)
        idx = row + j * DOC
        per = RETRIEVED // TILES
        picked = pos_ref[r, j // per, pl.ds(pl.multiple_of(j % per * PICK, PICK), PICK)]
        replaced = jnp.max(jnp.where(picked == idx, 1, 0), axis=0, keepdims=True)
        idx = jnp.where((row < length) & (replaced == 0), idx, FAR)
        pltpu.make_async_copy(arrays[0].at[0], buf.at[at], sem.at[at]).wait()

        def step(tile, wide):
            def get(ref):
                return ref[r, pl.ds(tile, wide)].reshape(wide * ROWS, HD)

            s = scores(r, tile, wide, buf[at, 0], idx)
            before = get(top_ref)
            top = jnp.maximum(before, jnp.max(s, axis=1, keepdims=True))
            fade = jnp.exp2((before - top) * EXP2)
            p, sums = weigh(s, top)
            put(top_ref, r, tile, wide, top)
            put(sum_ref, r, tile, wide, get(sum_ref) * fade + sums)
            value = jnp.dot(p, buf[at, 1], preferred_element_type=jnp.float32)
            put(acc, r, tile, wide, get(acc) * fade + value)

        tile = j // per

        @pl.when(tile % 2 == 1)
        def _():
            step(tile, 1)

        def pair(n, carry):
            step(n * 2, 2)
            return carry

        lax.fori_loop((tile + 1) // 2, TILES // 2, pair, 0)
        return carry

    lax.fori_loop(0, found, item, 0)

    if last:
        for r in range(count):
            for tile in range(TILES):
                sums = jnp.sum(sum_ref[r, tile], axis=1, keepdims=True)
                done = (acc[r, tile] / sums).astype(jnp.bfloat16)
                rows = slice(r * TOKENS + tile * SUB, r * TOKENS + (tile + 1) * SUB)
                for h in range(GROUP):
                    out_ref[rows, h * HD : (h + 1) * HD] = done[h * SUB : (h + 1) * SUB]


def attend(table, query, pos, extra, arrays, shifts, first, last):
    cands, count = CAP * len(arrays), query.shape[0]

    state = jax.ShapeDtypeStruct((count, TILES, ROWS, HD), jnp.float32)
    out_shape = [state] * 3
    if last:
        out_shape.append(jax.ShapeDtypeStruct((count * TOKENS, GROUP * HD), jnp.bfloat16))
    return pl.pallas_call(
        functools.partial(attend_kernel, shifts, count, first, last),
        out_shape=out_shape,
        in_specs=[SMEM] + [VMEM] * 5 + [ANY] * len(arrays),
        out_specs=[VMEM] * len(out_shape),
        scratch_shapes=[
            pltpu.VMEM((cands, 2, DOC, HD), jnp.bfloat16),
            pltpu.SMEM((cands,), jnp.int32),
            pltpu.SemaphoreType.DMA((cands,)),
        ],
        input_output_aliases={} if first else {3: 0, 4: 1, 5: 2},
        compiler_params=pltpu.CompilerParams(vmem_limit_bytes=ROOM),
        cost_estimate=pl.CostEstimate(
            flops=count * 2 * 1280 * 512 * 128 * len(arrays),
            bytes_accessed=count * ((4 << 20) + len(arrays) * (1 << 17)),
            transcendentals=count * 1280 * 512 * len(arrays) // 2,
        ),
        name="attend",
    )(table, query, pos, *extra, *arrays)


def project_kernel(spans, last, place_ref, w_ref, *refs):
    parts, refs = refs[: len(spans)], refs[len(spans) :]
    if last:
        before_ref, *refs = refs
    out_ref = refs[0]
    width = GROUP * HD
    rows = out_ref.shape[0]
    half = rows // 2
    for at in range(0, rows, half):
        total = before_ref[at : at + half] if last else None
        for part, (n, lo, hi) in zip(parts, spans):
            if lo <= at < hi:
                block = pl.ds(pl.multiple_of(place_ref[n] * width, width), width)
                term = jnp.dot(
                    part[at - lo : at - lo + half],
                    w_ref[block, :],
                    preferred_element_type=jnp.float32,
                )
                total = term if total is None else total + term
        out_ref[at : at + half] = total.astype(out_ref.dtype)


def project(place, pieces, w_out, before):
    spans, parts = [p[:3] for p in pieces], [p[3] for p in pieces]
    rows, columns = max(hi for _, _, hi in spans), w_out.shape[1]
    blocks, last = len({n for n, _, _ in spans}), before is not None
    return pl.pallas_call(
        functools.partial(project_kernel, spans, last),
        out_shape=jax.ShapeDtypeStruct((rows, columns), jnp.bfloat16 if last else jnp.float32),
        in_specs=[SMEM] + [VMEM] * (len(parts) + 1 + last),
        out_specs=VMEM,
        compiler_params=pltpu.CompilerParams(vmem_limit_bytes=PROJECT_ROOM),
        cost_estimate=pl.CostEstimate(
            flops=2 * rows * blocks * 512 * 512, bytes_accessed=blocks << 20, transcendentals=0
        ),
        name="project",
    )(place, w_out, *parts, *([before] if last else []))


def ring(block, by):
    return lax.ppermute(block, "tp", [(i, (i + 2 * by) % KVH) for i in range(KVH)])


def other_core(block):
    return lax.ppermute(block, "tp", [(i, i ^ 1) for i in range(KVH)])


def body(
    sel_hidden,
    norm_gain,
    w_query,
    w_key,
    w_value,
    w_out,
    doc_cache,
    home,
    doc_ids,
    doc_len,
    positions,
):
    me = lax.axis_index("grp").astype(jnp.int32).reshape(1)
    served = sel_hidden.shape[0]

    with jax.named_scope("pack"):
        scalars = [me, home, doc_ids.reshape(-1), doc_len]
        *early, table = pack(first_pack_kernel, EARLY, scalars, doc_cache, True)
        late = list(pack(second_pack_kernel, LATE, [table], doc_cache, False))
        packed = {b[0]: p for b, p in zip(EARLY + LATE, early + late)}

    with jax.named_scope("positions"):
        new_index = jnp.pad(
            positions, ((0, 0), (0, PADDED - TOKENS)), constant_values=FAR
        ).reshape(served, 1, PADDED)
        row_pos = jnp.broadcast_to(
            positions.reshape(served, TILES, 1, SUB), (served, TILES, GROUP, SUB)
        ).reshape(served, TILES, ROWS, 1)

    with jax.named_scope("projections"):
        xf = sel_hidden.astype(jnp.float32)
        normed = (
            xf * lax.rsqrt(jnp.mean(xf * xf, axis=-1, keepdims=True) + 1e-05) * norm_gain
        ).astype(jnp.bfloat16)
        normed_rows = normed.reshape(served * TOKENS, normed.shape[2])

        def dot(w):
            out = jnp.dot(normed_rows, w, preferred_element_type=jnp.float32)
            return out.astype(jnp.bfloat16).reshape(served, TOKENS, w.shape[1])

        query, key_new, value_new = dot(w_query), dot(w_key), dot(w_value)
        pad = ((0, 0), (0, PADDED - TOKENS), (0, 0))
        key_new, value_new = jnp.pad(key_new, pad), jnp.pad(value_new, pad)

    arrived = {(0, 0): doc_cache}

    def after(blocks, *done):
        return lax.optimization_barrier((blocks, done))[0]

    def send(names, blocks, hops):
        with jax.named_scope("documents"):
            for s, block, hop in zip(names, blocks, hops):
                arrived[s] = shift(block, hop)

    def attention(n, state):
        shifts, last = STAGES[n], n == len(STAGES) - 1
        with jax.named_scope("attention"):
            return attend(
                table,
                query,
                row_pos,
                state,
                [arrived[s] for s in shifts],
                shifts,
                n == 0,
                last,
            )

    send(TWO, [packed[s] for s in TWO], TWO)
    send(DIAGONAL, [packed[s] for s in DIAGONAL], DIAGONAL)
    state = attention(0, [new_index, key_new, value_new])
    now = NEAR + OPPOSITE
    send(now, after([packed[s] for s in now], [arrived[s] for s in TWO], state), now)
    state = attention(1, state)
    blocks = []
    for s in KNIGHT:
        through = (0, 2) if s[1] == 2 else (2, 0)
        at = CAP * CARRIED[through].index(s)
        blocks.append(arrived[through][at : at + CAP])
    send(KNIGHT, after(blocks, [arrived[s] for s in DIAGONAL], state), NEAR)
    state = attention(2, state)
    state = attention(3, state)
    own = attention(len(STAGES) - 1, state)[-1]

    with jax.named_scope("output"):
        tp = lax.axis_index("tp")
        z, core = tp // 2, tp % 2
        planes = jnp.stack([z, (z + 3) % SIDE, (z + 1) % SIDE, (z + 2) % SIDE])
        place = jnp.concatenate([planes * 2 + core, planes * 2 + 1 - core]).astype(jnp.int32)
        rows = served * TOKENS
        half = rows // 2
        up, down, core = ring(own, 1), ring(own, -1), other_core(own)
        near = [(0, own), (4, core), (1, up), (2, down), (5, other_core(up)), (6, other_core(down))]
        near = [(n, 0, rows, p) for n, p in near]
        far = [ring(up[:half], 1), ring(down[half:], -1)]
        partial = project(place, near, w_out, None)
        far = lax.optimization_barrier((far, partial))[0]
        cross = [other_core(p) for p in far]
        pieces = [(3, 0, half, far[0]), (3, half, rows, far[1])]
        pieces += [(7, 0, half, cross[0]), (7, half, rows, cross[1])]
        mixed = project(place, pieces, w_out, partial)
        return mixed.reshape(served, TOKENS, w_out.shape[1])


def solution(mesh):
    return jax.shard_map(
        body,
        mesh=mesh,
        in_specs=(
            P("grp", None, None),
            P(),
            P(None, "tp"),
            P(None, "tp"),
            P(None, "tp"),
            P(None, "tp"),
            P("grp", None, None, "tp"),
            P(),
            P(),
            P(),
            P("grp", None),
        ),
        out_specs=P("grp", None, "tp"),
        check_vma=False,
    )
```

```python
import functools
import math

import jax
import jax.numpy as jnp
from jax import lax
from jax.experimental import pallas as pl
from jax.experimental.pallas import tpu as pltpu
from jax.sharding import PartitionSpec as P

H = 32
KVH = 8
HD = 128
CAP = 2
GROUP = H // KVH
SIDE = 4
GROUPS = 16
STORED = 16
SLOTS = 16
PICK = 40
DOC = 512
TOKENS = 320
RETRIEVED = 8
TILES = 4
SUB = TOKENS // TILES
ROWS = SUB * GROUP
PADDED = 384
FAR = 2**30
EXP2 = HD ** (-0.5) * math.log2(math.e)

NEAR = [(1, 0), (3, 0), (0, 1), (0, 3)]
DIAGONAL = [(1, 1), (3, 3), (1, 3), (3, 1)]
OPPOSITE = [(2, 2)]
KNIGHT = [(1, 2), (3, 2), (2, 1), (2, 3)]
TWO = [(2, 0), (0, 2)]
CARRIED = {(2, 0): [(2, 0), (2, 1), (2, 3)], (0, 2): [(0, 2), (1, 2), (3, 2)]}
EARLY = [CARRIED[s] for s in TWO]
LATE = [[s] for s in DIAGONAL + NEAR + OPPOSITE]
CHOSEN = GROUPS * CAP + 2 * SLOTS
STAGES = [[(0, 0)], TWO, DIAGONAL, NEAR + OPPOSITE, KNIGHT]
JOINED = []
ROOM = 24 << 20
ALL_ROOM = 56 << 20
PROJECT_ROOM = 24 << 20

ANY = pl.BlockSpec(memory_space=pl.ANY)
HBM = pl.BlockSpec(memory_space=pltpu.HBM)
VMEM = pl.BlockSpec(memory_space=pltpu.VMEM)
SMEM = pl.BlockSpec(memory_space=pltpu.SMEM)


def shift(block, by):
    pairs = [
        (x * SIDE + y, (x + by[0]) % SIDE * SIDE + (y + by[1]) % SIDE)
        for x in range(SIDE)
        for y in range(SIDE)
    ]
    return lax.ppermute(block, "grp", pairs)


def copy_chosen(table_ref, cache_ref, blocks, out_refs, stage, read_sem, write_sem, between):
    me = table_ref[CHOSEN + GROUPS * CAP]
    x, y = me // SIDE, me % SIDE

    def each(act):
        at = 0
        for block, out in zip(blocks, out_refs):
            for n, (dx, dy) in enumerate(block):
                g = (x + dx) % SIDE * SIDE + (y + dy) % SIDE
                for k in range(CAP):
                    doc = table_ref[CHOSEN + g * CAP + k]

                    @pl.when(doc >= 0)
                    def _(at=at, doc=doc, out=out.at[n * CAP + k]):
                        act(at, doc, out)

                    at += 1

    def read(at, doc):
        return pltpu.make_async_copy(cache_ref.at[doc], stage.at[at], read_sem.at[at])

    def write(at, out):
        return pltpu.make_async_copy(stage.at[at], out, write_sem.at[at])

    def forward(at, doc, out):
        read(at, doc).wait()
        write(at, out).start()

    each(lambda at, doc, out: read(at, doc).start())
    between()
    each(forward)
    each(lambda at, doc, out: write(at, out).wait())


def first_pack_kernel(me_ref, home_ref, ids_ref, len_ref, cache_ref, *refs):
    out_refs, (table_ref, *scratch) = refs[: len(EARLY)], refs[len(EARLY) :]
    me = me_ref[0]

    x, y = me // SIDE, me % SIDE

    def outgoing(g, carry):
        one, two = jnp.int32(-1), jnp.int32(-1)
        for i in range(SLOTS):
            slot = home_ref[ids_ref[g * SLOTS + i]] - me * STORED
            hit = (slot >= 0) & (slot < STORED)
            two = jnp.where(hit, one, two)
            one = jnp.where(hit, slot, one)
        table_ref[CHOSEN + g * CAP] = jnp.where(two >= 0, two, one)
        table_ref[CHOSEN + g * CAP + 1] = jnp.where(two >= 0, one, -1)
        return carry

    for block in EARLY:
        for dx, dy in block:
            outgoing((x + dx) % SIDE * SIDE + (y + dy) % SIDE, 0)
    table_ref[CHOSEN + GROUPS * CAP] = me

    def rest():
        lax.fori_loop(0, GROUPS, outgoing, 0)
        for at in range(GROUPS * CAP):
            table_ref[at] = jnp.int32(-1)
        for i in range(SLOTS):
            doc = ids_ref[me * SLOTS + i]
            location = home_ref[doc]
            at = location // STORED * CAP
            table_ref[at + jnp.where(table_ref[at] >= 0, 1, 0)] = jnp.int32(i)
            table_ref[GROUPS * CAP + i] = location % STORED
            table_ref[GROUPS * CAP + SLOTS + i] = len_ref[doc]

    copy_chosen(table_ref, cache_ref, EARLY, out_refs, *scratch, rest)


def second_pack_kernel(table_ref, cache_ref, *refs):
    out_refs, scratch = refs[: len(LATE)], refs[len(LATE) :]
    copy_chosen(table_ref, cache_ref, LATE, out_refs, *scratch, lambda: None)


def pack(kernel, blocks, scalars, cache, with_table):
    shapes = [(CAP * len(b), 2, DOC, HD) for b in blocks]
    total = sum(s[0] for s in shapes)
    table = [jax.ShapeDtypeStruct((CHOSEN + GROUPS * CAP + 1,), jnp.int32)] if with_table else []
    return pl.pallas_call(
        kernel,
        out_shape=[jax.ShapeDtypeStruct(s, jnp.bfloat16) for s in shapes] + table,
        in_specs=[SMEM] * len(scalars) + [HBM],
        out_specs=[HBM] * len(blocks) + [SMEM] * len(table),
        scratch_shapes=[
            pltpu.VMEM((total, 2, DOC, HD), jnp.bfloat16),
            pltpu.SemaphoreType.DMA((total,)),
            pltpu.SemaphoreType.DMA((total,)),
        ],
        compiler_params=pltpu.CompilerParams(vmem_limit_bytes=ALL_ROOM),
        cost_estimate=pl.CostEstimate(flops=0, bytes_accessed=5 << 20, transcendentals=0),
        name="pack",
    )(*scalars, cache)


def attend_kernel(shifts, count, first, last, *refs):
    refs = list(refs)
    table_ref, q_ref, pos_ref = refs[:3]
    if first:
        new_idx_ref, new_k_ref, new_v_ref = refs[3:6]
    arrays, refs = refs[6 : 6 + len(shifts)], refs[6 + len(shifts) :]
    acc, top_ref, sum_ref, *refs = refs
    if last:
        out_ref, *refs = refs
    buf, items, sem = refs
    me = table_ref[CHOSEN + GROUPS * CAP]
    x, y = me // SIDE, me % SIDE

    found = jnp.int32(0)
    for (dx, dy), array in zip(shifts, arrays):
        skip = CAP if (dx, dy) in JOINED else 0
        source = (x - dx + SIDE) % SIDE * SIDE + (y - dy + SIDE) % SIDE
        for k in range(CAP):
            i = table_ref[source * CAP + k]
            mine = i >= 0

            @pl.when(mine)
            def _(i=i, array=array, k=k, at=found, own=(dx, dy) == (0, 0)):
                where = table_ref[GROUPS * CAP + i] if own else k + skip
                items[at] = i
                pltpu.make_async_copy(array.at[where], buf.at[at], sem.at[at]).start()

            found = found + jnp.where(mine, 1, 0)

    def scores(r, tile, wide, keys, idx):
        q = []
        for n in range(wide):
            rows = pl.ds(pl.multiple_of((tile + n) * SUB, SUB), SUB)
            q += [q_ref[r, rows, h * HD : (h + 1) * HD] for h in range(GROUP)]
        s = lax.dot_general(
            jnp.concatenate(q, axis=0),
            keys,
            (((1,), (1,)), ((), ())),
            preferred_element_type=jnp.float32,
        )
        pos = pos_ref[r, pl.ds(tile, wide)].reshape(wide * ROWS, 1)
        return jnp.where(idx <= pos, s, -1e30)

    def weigh(s, top):
        p = jnp.exp2((s - jnp.concatenate([top] * (s.shape[1] // HD), axis=1)) * EXP2)
        parts = [p[:, c : c + HD] for c in range(0, s.shape[1], HD)]
        return p.astype(jnp.bfloat16), functools.reduce(jnp.add, parts)

    def put(ref, r, tile, wide, value):
        ref[r, pl.ds(tile, wide)] = value.reshape(wide, ROWS, HD)

    if first:

        def start(at, carry):
            r, tile = at // (TILES // 2), at % (TILES // 2) * 2
            s = scores(r, tile, 2, new_k_ref[r], new_idx_ref[r])
            top = jnp.broadcast_to(jnp.max(s, axis=1, keepdims=True), (2 * ROWS, HD))
            p, sums = weigh(s, top)
            put(top_ref, r, tile, 2, top)
            put(sum_ref, r, tile, 2, sums)
            value = jnp.dot(p, new_v_ref[r], preferred_element_type=jnp.float32)
            put(acc, r, tile, 2, value)
            return carry

        lax.fori_loop(0, count * TILES // 2, start, 0)

    def item(at, carry):
        i = items[at]
        r, j = i // RETRIEVED, i % RETRIEVED
        length = table_ref[GROUPS * CAP + SLOTS + i]
        row = lax.broadcasted_iota(jnp.int32, (1, DOC), 1)
        idx = row + j * DOC
        per = RETRIEVED // TILES
        picked = pos_ref[r, j // per, pl.ds(pl.multiple_of(j % per * PICK, PICK), PICK)]
        replaced = jnp.max(jnp.where(picked == idx, 1, 0), axis=0, keepdims=True)
        idx = jnp.where((row < length) & (replaced == 0), idx, FAR)
        pltpu.make_async_copy(arrays[0].at[0], buf.at[at], sem.at[at]).wait()

        bias = jnp.where(idx < FAR, 0.0, -1e30)

        def step(tile):
            wide = TILES - tile

            def get(ref):
                return ref[r, tile:].reshape(wide * ROWS, HD)

            q = []
            for n in range(tile, TILES):
                rows = slice(n * SUB, (n + 1) * SUB)
                q += [q_ref[r, rows, h * HD : (h + 1) * HD] for h in range(GROUP)]
            s = lax.dot_general(
                jnp.concatenate(q, axis=0),
                buf[at, 0],
                (((1,), (1,)), ((), ())),
                preferred_element_type=jnp.float32,
            )
            within = jnp.where(idx <= pos_ref[r, tile], s[:ROWS], -1e30)
            s = jnp.concatenate([within, s[ROWS:] + bias], axis=0) if wide > 1 else within
            before = get(top_ref)
            top = jnp.maximum(before, jnp.max(s, axis=1, keepdims=True))
            fade = jnp.exp2((before - top) * EXP2)
            p, sums = weigh(s, top)
            value = jnp.dot(p, buf[at, 1], preferred_element_type=jnp.float32)
            shape = (wide, ROWS, HD)
            top_ref[r, tile:] = top.reshape(shape)
            sum_ref[r, tile:] = (get(sum_ref) * fade + sums).reshape(shape)
            acc[r, tile:] = (get(acc) * fade + value).reshape(shape)

        for tile in range(TILES):
            pl.when(j // per == tile)(functools.partial(step, tile))
        return carry

    lax.fori_loop(0, found, item, 0)

    if last:
        for r in range(count):
            for tile in range(TILES):
                sums = jnp.sum(sum_ref[r, tile], axis=1, keepdims=True)
                done = (acc[r, tile] / sums).astype(jnp.bfloat16)
                rows = slice(r * TOKENS + tile * SUB, r * TOKENS + (tile + 1) * SUB)
                for h in range(GROUP):
                    out_ref[rows, h * HD : (h + 1) * HD] = done[h * SUB : (h + 1) * SUB]


def attend(table, query, pos, extra, arrays, shifts, first, last):
    cands, count = CAP * len(arrays), query.shape[0]

    state = jax.ShapeDtypeStruct((count, TILES, ROWS, HD), jnp.float32)
    out_shape = [state] * 3
    if last:
        out_shape.append(jax.ShapeDtypeStruct((count * TOKENS, GROUP * HD), jnp.bfloat16))
    return pl.pallas_call(
        functools.partial(attend_kernel, shifts, count, first, last),
        out_shape=out_shape,
        in_specs=[SMEM] + [VMEM] * 5 + [ANY] * len(arrays),
        out_specs=[VMEM] * len(out_shape),
        scratch_shapes=[
            pltpu.VMEM((cands, 2, DOC, HD), jnp.bfloat16),
            pltpu.SMEM((cands,), jnp.int32),
            pltpu.SemaphoreType.DMA((cands,)),
        ],
        input_output_aliases={} if first else {3: 0, 4: 1, 5: 2},
        compiler_params=pltpu.CompilerParams(vmem_limit_bytes=ROOM),
        cost_estimate=pl.CostEstimate(
            flops=count * 2 * 1280 * 512 * 128 * len(arrays),
            bytes_accessed=count * ((4 << 20) + len(arrays) * (1 << 17)),
            transcendentals=count * 1280 * 512 * len(arrays) // 2,
        ),
        name="attend",
    )(table, query, pos, *extra, *arrays)


def project_kernel(spans, last, place_ref, w_ref, *refs):
    parts, refs = refs[: len(spans)], refs[len(spans) :]
    if last:
        before_ref, *refs = refs
    out_ref = refs[0]
    width = GROUP * HD
    rows = out_ref.shape[0]
    half = rows // 2
    for at in range(0, rows, half):
        total = before_ref[at : at + half] if last else None
        for part, (n, lo, hi) in zip(parts, spans):
            if lo <= at < hi:
                block = pl.ds(pl.multiple_of(place_ref[n] * width, width), width)
                term = jnp.dot(
                    part[at - lo : at - lo + half],
                    w_ref[block, :],
                    preferred_element_type=jnp.float32,
                )
                total = term if total is None else total + term
        out_ref[at : at + half] = total.astype(out_ref.dtype)


def project(place, pieces, w_out, before):
    spans, parts = [p[:3] for p in pieces], [p[3] for p in pieces]
    rows, columns = max(hi for _, _, hi in spans), w_out.shape[1]
    blocks, last = len({n for n, _, _ in spans}), before is not None
    return pl.pallas_call(
        functools.partial(project_kernel, spans, last),
        out_shape=jax.ShapeDtypeStruct((rows, columns), jnp.bfloat16 if last else jnp.float32),
        in_specs=[SMEM] + [VMEM] * (len(parts) + 1 + last),
        out_specs=VMEM,
        compiler_params=pltpu.CompilerParams(vmem_limit_bytes=PROJECT_ROOM),
        cost_estimate=pl.CostEstimate(
            flops=2 * rows * blocks * 512 * 512, bytes_accessed=blocks << 20, transcendentals=0
        ),
        name="project",
    )(place, w_out, *parts, *([before] if last else []))


def ring(block, by):
    return lax.ppermute(block, "tp", [(i, (i + 2 * by) % KVH) for i in range(KVH)])


def other_core(block):
    return lax.ppermute(block, "tp", [(i, i ^ 1) for i in range(KVH)])


def body(
    sel_hidden,
    norm_gain,
    w_query,
    w_key,
    w_value,
    w_out,
    doc_cache,
    home,
    doc_ids,
    doc_len,
    positions,
):
    me = lax.axis_index("grp").astype(jnp.int32).reshape(1)
    served = sel_hidden.shape[0]

    with jax.named_scope("pack"):
        scalars = [me, home, doc_ids.reshape(-1), doc_len]
        *early, table = pack(first_pack_kernel, EARLY, scalars, doc_cache, True)
        late = list(pack(second_pack_kernel, LATE, [table], doc_cache, False))
        packed = {b[0]: p for b, p in zip(EARLY + LATE, early + late)}

    with jax.named_scope("positions"):
        new_index = jnp.pad(
            positions, ((0, 0), (0, PADDED - TOKENS)), constant_values=FAR
        ).reshape(served, 1, PADDED)
        row_pos = jnp.broadcast_to(
            positions.reshape(served, TILES, 1, SUB), (served, TILES, GROUP, SUB)
        ).reshape(served, TILES, ROWS, 1)

    with jax.named_scope("projections"):
        xf = sel_hidden.astype(jnp.float32)
        normed = (
            xf * lax.rsqrt(jnp.mean(xf * xf, axis=-1, keepdims=True) + 1e-05) * norm_gain
        ).astype(jnp.bfloat16)
        normed_rows = normed.reshape(served * TOKENS, normed.shape[2])

        def dot(w):
            out = jnp.dot(normed_rows, w, preferred_element_type=jnp.float32)
            return out.astype(jnp.bfloat16).reshape(served, TOKENS, w.shape[1])

        query, key_new, value_new = dot(w_query), dot(w_key), dot(w_value)
        pad = ((0, 0), (0, PADDED - TOKENS), (0, 0))
        key_new, value_new = jnp.pad(key_new, pad), jnp.pad(value_new, pad)

    arrived = {(0, 0): doc_cache}

    def after(blocks, *done):
        return lax.optimization_barrier((blocks, done))[0]

    def send(names, blocks, hops):
        with jax.named_scope("documents"):
            for s, block, hop in zip(names, blocks, hops):
                arrived[s] = shift(block, hop)

    def attention(n, state):
        shifts, last = STAGES[n], n == len(STAGES) - 1
        with jax.named_scope("attention"):
            return attend(
                table,
                query,
                row_pos,
                state,
                [arrived[s] for s in shifts],
                shifts,
                n == 0,
                last,
            )

    send(TWO, [packed[s] for s in TWO], TWO)
    send(DIAGONAL, [packed[s] for s in DIAGONAL], DIAGONAL)
    state = attention(0, [new_index, key_new, value_new])
    now = NEAR + OPPOSITE
    send(now, after([packed[s] for s in now], [arrived[s] for s in TWO], state), now)
    state = attention(1, state)
    blocks = []
    for s in KNIGHT:
        through = (0, 2) if s[1] == 2 else (2, 0)
        at = CAP * CARRIED[through].index(s)
        blocks.append(arrived[through][at : at + CAP])
    send(KNIGHT, after(blocks, [arrived[s] for s in DIAGONAL], state), NEAR)
    state = attention(2, state)
    state = attention(3, state)
    own = attention(len(STAGES) - 1, state)[-1]

    with jax.named_scope("output"):
        tp = lax.axis_index("tp")
        z, core = tp // 2, tp % 2
        planes = jnp.stack([z, (z + 3) % SIDE, (z + 1) % SIDE, (z + 2) % SIDE])
        place = jnp.concatenate([planes * 2 + core, planes * 2 + 1 - core]).astype(jnp.int32)
        rows = served * TOKENS
        half = rows // 2
        up, down, core = ring(own, 1), ring(own, -1), other_core(own)
        near = [(0, own), (4, core), (1, up), (2, down), (5, other_core(up)), (6, other_core(down))]
        near = [(n, 0, rows, p) for n, p in near]
        far = [ring(up[:half], 1), ring(down[half:], -1)]
        partial = project(place, near, w_out, None)
        far = lax.optimization_barrier((far, partial))[0]
        cross = [other_core(p) for p in far]
        pieces = [(3, 0, half, far[0]), (3, half, rows, far[1])]
        pieces += [(7, 0, half, cross[0]), (7, half, rows, cross[1])]
        mixed = project(place, pieces, w_out, partial)
        return mixed.reshape(served, TOKENS, w_out.shape[1])


def solution(mesh):
    return jax.shard_map(
        body,
        mesh=mesh,
        in_specs=(
            P("grp", None, None),
            P(),
            P(None, "tp"),
            P(None, "tp"),
            P(None, "tp"),
            P(None, "tp"),
            P("grp", None, None, "tp"),
            P(),
            P(),
            P(),
            P("grp", None),
        ),
        out_specs=P("grp", None, "tp"),
        check_vma=False,
    )
```

```python
import functools
import math

import jax
import jax.numpy as jnp
from jax import lax
from jax.experimental import pallas as pl
from jax.experimental.pallas import tpu as pltpu
from jax.sharding import PartitionSpec as P

H = 32
KVH = 8
HD = 128
CAP = 2
GROUP = H // KVH
SIDE = 4
GROUPS = 16
STORED = 16
SLOTS = 16
SERVED = 2
PICK = 40
DOC = 512
TOKENS = 320
RETRIEVED = 8
TILES = 4
SUB = TOKENS // TILES
ROWS = SUB * GROUP
PADDED = 384
FAR = 2**30
EXP2 = HD ** (-0.5) * math.log2(math.e)

NEAR = [(1, 0), (3, 0), (0, 1), (0, 3)]
DIAGONAL = [(1, 1), (3, 3), (1, 3), (3, 1)]
OPPOSITE = [(2, 2)]
KNIGHT = [(1, 2), (3, 2), (2, 1), (2, 3)]
TWO = [(2, 0), (0, 2)]
CARRIED = {(2, 0): [(2, 0), (2, 1), (2, 3)], (0, 2): [(0, 2), (1, 2), (3, 2)]}
EARLY = [CARRIED[s] for s in TWO]
LATE = [[s] for s in DIAGONAL + NEAR + OPPOSITE]
CHOSEN = GROUPS * CAP + 2 * SLOTS
STAGES = [[(0, 0)], TWO, DIAGONAL, NEAR + OPPOSITE, KNIGHT]
JOINED = []
ROOM = 24 << 20
ALL_ROOM = 56 << 20
PROJECT_ROOM = 24 << 20

ANY = pl.BlockSpec(memory_space=pl.ANY)
HBM = pl.BlockSpec(memory_space=pltpu.HBM)
VMEM = pl.BlockSpec(memory_space=pltpu.VMEM)
SMEM = pl.BlockSpec(memory_space=pltpu.SMEM)


def shift(block, by):
    pairs = [
        (x * SIDE + y, (x + by[0]) % SIDE * SIDE + (y + by[1]) % SIDE)
        for x in range(SIDE)
        for y in range(SIDE)
    ]
    return lax.ppermute(block, "grp", pairs)


def copy_chosen(table_ref, cache_ref, blocks, out_refs, stage, read_sem, write_sem, between):
    me = table_ref[CHOSEN + GROUPS * CAP]
    x, y = me // SIDE, me % SIDE

    def each(act):
        at = 0
        for block, out in zip(blocks, out_refs):
            for n, (dx, dy) in enumerate(block):
                g = (x + dx) % SIDE * SIDE + (y + dy) % SIDE
                for k in range(CAP):
                    doc = table_ref[CHOSEN + g * CAP + k]

                    @pl.when(doc >= 0)
                    def _(at=at, doc=doc, out=out.at[n * CAP + k]):
                        act(at, doc, out)

                    at += 1

    def read(at, doc):
        return pltpu.make_async_copy(cache_ref.at[doc], stage.at[at], read_sem.at[at])

    def write(at, out):
        return pltpu.make_async_copy(stage.at[at], out, write_sem.at[at])

    def forward(at, doc, out):
        read(at, doc).wait()
        write(at, out).start()

    each(lambda at, doc, out: read(at, doc).start())
    between()
    each(forward)
    each(lambda at, doc, out: write(at, out).wait())


def first_pack_kernel(me_ref, home_ref, ids_ref, len_ref, cache_ref, *refs):
    out_refs, (table_ref, *scratch) = refs[: len(EARLY)], refs[len(EARLY) :]
    me = me_ref[0]

    x, y = me // SIDE, me % SIDE

    def outgoing(g, carry):
        one, two = jnp.int32(-1), jnp.int32(-1)
        for i in range(SLOTS):
            slot = home_ref[ids_ref[i % RETRIEVED, g * SERVED + i // RETRIEVED]] - me * STORED
            hit = (slot >= 0) & (slot < STORED)
            two = jnp.where(hit, one, two)
            one = jnp.where(hit, slot, one)
        table_ref[CHOSEN + g * CAP] = jnp.where(two >= 0, two, one)
        table_ref[CHOSEN + g * CAP + 1] = jnp.where(two >= 0, one, -1)
        return carry

    for block in EARLY:
        for dx, dy in block:
            outgoing((x + dx) % SIDE * SIDE + (y + dy) % SIDE, 0)
    table_ref[CHOSEN + GROUPS * CAP] = me

    def rest():
        lax.fori_loop(0, GROUPS, outgoing, 0)
        for at in range(GROUPS * CAP):
            table_ref[at] = jnp.int32(-1)
        for i in range(SLOTS):
            doc = ids_ref[i % RETRIEVED, me * SERVED + i // RETRIEVED]
            location = home_ref[doc]
            at = location // STORED * CAP
            table_ref[at + jnp.where(table_ref[at] >= 0, 1, 0)] = jnp.int32(i)
            table_ref[GROUPS * CAP + i] = location % STORED
            table_ref[GROUPS * CAP + SLOTS + i] = len_ref[doc]

    copy_chosen(table_ref, cache_ref, EARLY, out_refs, *scratch, rest)


def second_pack_kernel(table_ref, cache_ref, *refs):
    out_refs, scratch = refs[: len(LATE)], refs[len(LATE) :]
    copy_chosen(table_ref, cache_ref, LATE, out_refs, *scratch, lambda: None)


def pack(kernel, blocks, scalars, cache, with_table):
    shapes = [(CAP * len(b), 2, DOC, HD) for b in blocks]
    total = sum(s[0] for s in shapes)
    table = [jax.ShapeDtypeStruct((CHOSEN + GROUPS * CAP + 1,), jnp.int32)] if with_table else []
    return pl.pallas_call(
        kernel,
        out_shape=[jax.ShapeDtypeStruct(s, jnp.bfloat16) for s in shapes] + table,
        in_specs=[SMEM] * len(scalars) + [HBM],
        out_specs=[HBM] * len(blocks) + [SMEM] * len(table),
        scratch_shapes=[
            pltpu.VMEM((total, 2, DOC, HD), jnp.bfloat16),
            pltpu.SemaphoreType.DMA((total,)),
            pltpu.SemaphoreType.DMA((total,)),
        ],
        compiler_params=pltpu.CompilerParams(vmem_limit_bytes=ALL_ROOM),
        cost_estimate=pl.CostEstimate(flops=0, bytes_accessed=5 << 20, transcendentals=0),
        name="pack",
    )(*scalars, cache)


def attend_kernel(shifts, count, first, last, *refs):
    refs = list(refs)
    table_ref, q_ref, pos_ref = refs[:3]
    if first:
        new_idx_ref, new_k_ref, new_v_ref = refs[3:6]
    arrays, refs = refs[6 : 6 + len(shifts)], refs[6 + len(shifts) :]
    acc, top_ref, sum_ref, *refs = refs
    if last:
        out_ref, *refs = refs
    buf, items, sem = refs
    me = table_ref[CHOSEN + GROUPS * CAP]
    x, y = me // SIDE, me % SIDE

    found = jnp.int32(0)
    for (dx, dy), array in zip(shifts, arrays):
        skip = CAP if (dx, dy) in JOINED else 0
        source = (x - dx + SIDE) % SIDE * SIDE + (y - dy + SIDE) % SIDE
        for k in range(CAP):
            i = table_ref[source * CAP + k]
            mine = i >= 0

            @pl.when(mine)
            def _(i=i, array=array, k=k, at=found, own=(dx, dy) == (0, 0)):
                where = table_ref[GROUPS * CAP + i] if own else k + skip
                items[at] = i
                pltpu.make_async_copy(array.at[where], buf.at[at], sem.at[at]).start()

            found = found + jnp.where(mine, 1, 0)

    def scores(r, tile, wide, keys, idx):
        q = []
        for n in range(wide):
            rows = pl.ds(pl.multiple_of((tile + n) * SUB, SUB), SUB)
            q += [q_ref[r, rows, h * HD : (h + 1) * HD] for h in range(GROUP)]
        s = lax.dot_general(
            jnp.concatenate(q, axis=0),
            keys,
            (((1,), (1,)), ((), ())),
            preferred_element_type=jnp.float32,
        )
        pos = pos_ref[r, pl.ds(tile, wide)].reshape(wide * ROWS, 1)
        return jnp.where(idx <= pos, s, -1e30)

    def weigh(s, top):
        p = jnp.exp2((s - jnp.concatenate([top] * (s.shape[1] // HD), axis=1)) * EXP2)
        parts = [p[:, c : c + HD] for c in range(0, s.shape[1], HD)]
        return p.astype(jnp.bfloat16), functools.reduce(jnp.add, parts)

    def put(ref, r, tile, wide, value):
        ref[r, pl.ds(tile, wide)] = value.reshape(wide, ROWS, HD)

    if first:

        def start(at, carry):
            r, tile = at // (TILES // 2), at % (TILES // 2) * 2
            s = scores(r, tile, 2, new_k_ref[r], new_idx_ref[r])
            top = jnp.broadcast_to(jnp.max(s, axis=1, keepdims=True), (2 * ROWS, HD))
            p, sums = weigh(s, top)
            put(top_ref, r, tile, 2, top)
            put(sum_ref, r, tile, 2, sums)
            value = jnp.dot(p, new_v_ref[r], preferred_element_type=jnp.float32)
            put(acc, r, tile, 2, value)
            return carry

        lax.fori_loop(0, count * TILES // 2, start, 0)

    def item(at, carry):
        i = items[at]
        r, j = i // RETRIEVED, i % RETRIEVED
        length = table_ref[GROUPS * CAP + SLOTS + i]
        row = lax.broadcasted_iota(jnp.int32, (1, DOC), 1)
        idx = row + j * DOC
        per = RETRIEVED // TILES
        picked = pos_ref[r, j // per, pl.ds(pl.multiple_of(j % per * PICK, PICK), PICK)]
        replaced = jnp.max(jnp.where(picked == idx, 1, 0), axis=0, keepdims=True)
        idx = jnp.where((row < length) & (replaced == 0), idx, FAR)
        pltpu.make_async_copy(arrays[0].at[0], buf.at[at], sem.at[at]).wait()

        bias = jnp.where(idx < FAR, 0.0, -1e30)

        def step(tile):
            wide = TILES - tile

            def get(ref):
                return ref[r, tile:].reshape(wide * ROWS, HD)

            q = []
            for n in range(tile, TILES):
                rows = slice(n * SUB, (n + 1) * SUB)
                q += [q_ref[r, rows, h * HD : (h + 1) * HD] for h in range(GROUP)]
            s = lax.dot_general(
                jnp.concatenate(q, axis=0),
                buf[at, 0],
                (((1,), (1,)), ((), ())),
                preferred_element_type=jnp.float32,
            )
            within = jnp.where(idx <= pos_ref[r, tile], s[:ROWS], -1e30)
            s = jnp.concatenate([within, s[ROWS:] + bias], axis=0) if wide > 1 else within
            before = get(top_ref)
            top = jnp.maximum(before, jnp.max(s, axis=1, keepdims=True))
            fade = jnp.exp2((before - top) * EXP2)
            p, sums = weigh(s, top)
            value = jnp.dot(p, buf[at, 1], preferred_element_type=jnp.float32)
            shape = (wide, ROWS, HD)
            top_ref[r, tile:] = top.reshape(shape)
            sum_ref[r, tile:] = (get(sum_ref) * fade + sums).reshape(shape)
            acc[r, tile:] = (get(acc) * fade + value).reshape(shape)

        for tile in range(TILES):
            pl.when(j // per == tile)(functools.partial(step, tile))
        return carry

    lax.fori_loop(0, found, item, 0)

    if last:
        for r in range(count):
            for tile in range(TILES):
                sums = jnp.sum(sum_ref[r, tile], axis=1, keepdims=True)
                done = (acc[r, tile] / sums).astype(jnp.bfloat16)
                rows = slice(r * TOKENS + tile * SUB, r * TOKENS + (tile + 1) * SUB)
                for h in range(GROUP):
                    out_ref[rows, h * HD : (h + 1) * HD] = done[h * SUB : (h + 1) * SUB]


def attend(table, query, pos, extra, arrays, shifts, first, last):
    cands, count = CAP * len(arrays), query.shape[0]

    state = jax.ShapeDtypeStruct((count, TILES, ROWS, HD), jnp.float32)
    out_shape = [state] * 3
    if last:
        out_shape.append(jax.ShapeDtypeStruct((count * TOKENS, GROUP * HD), jnp.bfloat16))
    return pl.pallas_call(
        functools.partial(attend_kernel, shifts, count, first, last),
        out_shape=out_shape,
        in_specs=[SMEM] + [VMEM] * 5 + [ANY] * len(arrays),
        out_specs=[VMEM] * len(out_shape),
        scratch_shapes=[
            pltpu.VMEM((cands, 2, DOC, HD), jnp.bfloat16),
            pltpu.SMEM((cands,), jnp.int32),
            pltpu.SemaphoreType.DMA((cands,)),
        ],
        input_output_aliases={} if first else {3: 0, 4: 1, 5: 2},
        compiler_params=pltpu.CompilerParams(vmem_limit_bytes=ROOM),
        cost_estimate=pl.CostEstimate(
            flops=count * 2 * 1280 * 512 * 128 * len(arrays),
            bytes_accessed=count * ((4 << 20) + len(arrays) * (1 << 17)),
            transcendentals=count * 1280 * 512 * len(arrays) // 2,
        ),
        name="attend",
    )(table, query, pos, *extra, *arrays)


def project_kernel(spans, last, place_ref, w_ref, *refs):
    parts, refs = refs[: len(spans)], refs[len(spans) :]
    if last:
        before_ref, *refs = refs
    out_ref = refs[0]
    width = GROUP * HD
    rows = out_ref.shape[0]
    half = rows // 2
    for at in range(0, rows, half):
        total = before_ref[at : at + half] if last else None
        for part, (n, lo, hi) in zip(parts, spans):
            if lo <= at < hi:
                block = pl.ds(pl.multiple_of(place_ref[n] * width, width), width)
                term = jnp.dot(
                    part[at - lo : at - lo + half],
                    w_ref[block, :],
                    preferred_element_type=jnp.float32,
                )
                total = term if total is None else total + term
        out_ref[at : at + half] = total.astype(out_ref.dtype)


def project(place, pieces, w_out, before):
    spans, parts = [p[:3] for p in pieces], [p[3] for p in pieces]
    rows, columns = max(hi for _, _, hi in spans), w_out.shape[1]
    blocks, last = len({n for n, _, _ in spans}), before is not None
    return pl.pallas_call(
        functools.partial(project_kernel, spans, last),
        out_shape=jax.ShapeDtypeStruct((rows, columns), jnp.bfloat16 if last else jnp.float32),
        in_specs=[SMEM] + [VMEM] * (len(parts) + 1 + last),
        out_specs=VMEM,
        compiler_params=pltpu.CompilerParams(vmem_limit_bytes=PROJECT_ROOM),
        cost_estimate=pl.CostEstimate(
            flops=2 * rows * blocks * 512 * 512, bytes_accessed=blocks << 20, transcendentals=0
        ),
        name="project",
    )(place, w_out, *parts, *([before] if last else []))


def ring(block, by):
    return lax.ppermute(block, "tp", [(i, (i + 2 * by) % KVH) for i in range(KVH)])


def other_core(block):
    return lax.ppermute(block, "tp", [(i, i ^ 1) for i in range(KVH)])


def body(
    sel_hidden,
    norm_gain,
    w_query,
    w_key,
    w_value,
    w_out,
    doc_cache,
    home,
    doc_ids,
    doc_len,
    positions,
):
    me = lax.axis_index("grp").astype(jnp.int32).reshape(1)
    served = sel_hidden.shape[0]

    with jax.named_scope("pack"):
        scalars = [me, home, doc_ids.T, doc_len]
        *early, table = pack(first_pack_kernel, EARLY, scalars, doc_cache, True)
        late = list(pack(second_pack_kernel, LATE, [table], doc_cache, False))
        packed = {b[0]: p for b, p in zip(EARLY + LATE, early + late)}

    with jax.named_scope("positions"):
        new_index = jnp.pad(
            positions, ((0, 0), (0, PADDED - TOKENS)), constant_values=FAR
        ).reshape(served, 1, PADDED)
        row_pos = jnp.broadcast_to(
            positions.reshape(served, TILES, 1, SUB), (served, TILES, GROUP, SUB)
        ).reshape(served, TILES, ROWS, 1)

    with jax.named_scope("projections"):
        xf = sel_hidden.astype(jnp.float32)
        normed = (
            xf * lax.rsqrt(jnp.mean(xf * xf, axis=-1, keepdims=True) + 1e-05) * norm_gain
        ).astype(jnp.bfloat16)
        normed_rows = normed.reshape(served * TOKENS, normed.shape[2])

        def dot(w):
            out = jnp.dot(normed_rows, w, preferred_element_type=jnp.float32)
            return out.astype(jnp.bfloat16).reshape(served, TOKENS, w.shape[1])

        query, key_new, value_new = dot(w_query), dot(w_key), dot(w_value)
        pad = ((0, 0), (0, PADDED - TOKENS), (0, 0))
        key_new, value_new = jnp.pad(key_new, pad), jnp.pad(value_new, pad)

    arrived = {(0, 0): doc_cache}

    def after(blocks, *done):
        return lax.optimization_barrier((blocks, done))[0]

    def send(names, blocks, hops):
        with jax.named_scope("documents"):
            for s, block, hop in zip(names, blocks, hops):
                arrived[s] = shift(block, hop)

    def attention(n, state):
        shifts, last = STAGES[n], n == len(STAGES) - 1
        with jax.named_scope("attention"):
            return attend(
                table,
                query,
                row_pos,
                state,
                [arrived[s] for s in shifts],
                shifts,
                n == 0,
                last,
            )

    send(TWO, [packed[s] for s in TWO], TWO)
    send(DIAGONAL, [packed[s] for s in DIAGONAL], DIAGONAL)
    state = attention(0, [new_index, key_new, value_new])
    now = NEAR + OPPOSITE
    send(now, after([packed[s] for s in now], [arrived[s] for s in TWO], state), now)
    state = attention(1, state)
    blocks = []
    for s in KNIGHT:
        through = (0, 2) if s[1] == 2 else (2, 0)
        at = CAP * CARRIED[through].index(s)
        blocks.append(arrived[through][at : at + CAP])
    send(KNIGHT[:1], after(blocks[:1], [arrived[s] for s in DIAGONAL], state), NEAR[:1])
    state = attention(2, state)
    send(KNIGHT[1:], after(blocks[1:], state), NEAR[1:])
    state = attention(3, state)
    own = attention(len(STAGES) - 1, state)[-1]

    with jax.named_scope("output"):
        tp = lax.axis_index("tp")
        z, core = tp // 2, tp % 2
        planes = jnp.stack([z, (z + 3) % SIDE, (z + 1) % SIDE, (z + 2) % SIDE])
        place = jnp.concatenate([planes * 2 + core, planes * 2 + 1 - core]).astype(jnp.int32)
        rows = served * TOKENS
        half = rows // 2
        up, down, core = ring(own, 1), ring(own, -1), other_core(own)
        near = [(0, own), (4, core), (1, up), (2, down), (5, other_core(up)), (6, other_core(down))]
        near = [(n, 0, rows, p) for n, p in near]
        far = [ring(up[:half], 1), ring(down[half:], -1)]
        partial = project(place, near, w_out, None)
        far = lax.optimization_barrier((far, partial))[0]
        cross = [other_core(p) for p in far]
        pieces = [(3, 0, half, far[0]), (3, half, rows, far[1])]
        pieces += [(7, 0, half, cross[0]), (7, half, rows, cross[1])]
        mixed = project(place, pieces, w_out, partial)
        return mixed.reshape(served, TOKENS, w_out.shape[1])


def solution(mesh):
    return jax.shard_map(
        body,
        mesh=mesh,
        in_specs=(
            P("grp", None, None),
            P(),
            P(None, "tp"),
            P(None, "tp"),
            P(None, "tp"),
            P(None, "tp"),
            P("grp", None, None, "tp"),
            P(),
            P(),
            P(),
            P("grp", None),
        ),
        out_specs=P("grp", None, "tp"),
        check_vma=False,
    )
```

```python
import functools
import math

import jax
import jax.numpy as jnp
from jax import lax
from jax.experimental import pallas as pl
from jax.experimental.pallas import tpu as pltpu
from jax.sharding import PartitionSpec as P

H = 32
KVH = 8
HD = 128
CAP = 2
GROUP = H // KVH
SIDE = 4
GROUPS = 16
STORED = 16
SLOTS = 16
SERVED = 2
PICK = 40
DOC = 512
TOKENS = 320
RETRIEVED = 8
TILES = 4
SUB = TOKENS // TILES
ROWS = SUB * GROUP
PADDED = 384
FAR = 2**30
EXP2 = HD ** (-0.5) * math.log2(math.e)

NEAR = [(1, 0), (3, 0), (0, 1), (0, 3)]
DIAGONAL = [(1, 1), (3, 3), (1, 3), (3, 1)]
OPPOSITE = [(2, 2)]
KNIGHT = [(1, 2), (3, 2), (2, 1), (2, 3)]
TWO = [(2, 0), (0, 2)]
CARRIED = {(2, 0): [(2, 0), (2, 1), (2, 3)], (0, 2): [(0, 2), (1, 2), (3, 2)]}
EARLY = [CARRIED[s] for s in TWO]
LATE = [[s] for s in DIAGONAL + NEAR + OPPOSITE]
CHOSEN = GROUPS * CAP + 2 * SLOTS
STAGES = [[(0, 0)], DIAGONAL, TWO + NEAR + OPPOSITE, KNIGHT]
JOINED = []
ROOM = 24 << 20
ALL_ROOM = 56 << 20
PROJECT_ROOM = 24 << 20

ANY = pl.BlockSpec(memory_space=pl.ANY)
HBM = pl.BlockSpec(memory_space=pltpu.HBM)
VMEM = pl.BlockSpec(memory_space=pltpu.VMEM)
SMEM = pl.BlockSpec(memory_space=pltpu.SMEM)


def shift(block, by):
    pairs = [
        (x * SIDE + y, (x + by[0]) % SIDE * SIDE + (y + by[1]) % SIDE)
        for x in range(SIDE)
        for y in range(SIDE)
    ]
    return lax.ppermute(block, "grp", pairs)


def copy_chosen(table_ref, cache_ref, blocks, out_refs, stage, read_sem, write_sem, between):
    me = table_ref[CHOSEN + GROUPS * CAP]
    x, y = me // SIDE, me % SIDE

    def each(act):
        at = 0
        for block, out in zip(blocks, out_refs):
            for n, (dx, dy) in enumerate(block):
                g = (x + dx) % SIDE * SIDE + (y + dy) % SIDE
                for k in range(CAP):
                    doc = table_ref[CHOSEN + g * CAP + k]

                    @pl.when(doc >= 0)
                    def _(at=at, doc=doc, out=out.at[n * CAP + k]):
                        act(at, doc, out)

                    at += 1

    def read(at, doc):
        return pltpu.make_async_copy(cache_ref.at[doc], stage.at[at], read_sem.at[at])

    def write(at, out):
        return pltpu.make_async_copy(stage.at[at], out, write_sem.at[at])

    def forward(at, doc, out):
        read(at, doc).wait()
        write(at, out).start()

    each(lambda at, doc, out: read(at, doc).start())
    between()
    each(forward)
    each(lambda at, doc, out: write(at, out).wait())


def first_pack_kernel(me_ref, home_ref, ids_ref, len_ref, cache_ref, *refs):
    out_refs, (table_ref, *scratch) = refs[: len(EARLY)], refs[len(EARLY) :]
    me = me_ref[0]

    x, y = me // SIDE, me % SIDE

    def outgoing(g, carry):
        one, two = jnp.int32(-1), jnp.int32(-1)
        for i in range(SLOTS):
            slot = home_ref[ids_ref[i % RETRIEVED, g * SERVED + i // RETRIEVED]] - me * STORED
            hit = (slot >= 0) & (slot < STORED)
            two = jnp.where(hit, one, two)
            one = jnp.where(hit, slot, one)
        table_ref[CHOSEN + g * CAP] = jnp.where(two >= 0, two, one)
        table_ref[CHOSEN + g * CAP + 1] = jnp.where(two >= 0, one, -1)
        return carry

    for block in EARLY:
        for dx, dy in block:
            outgoing((x + dx) % SIDE * SIDE + (y + dy) % SIDE, 0)
    table_ref[CHOSEN + GROUPS * CAP] = me

    def rest():
        lax.fori_loop(0, GROUPS, outgoing, 0)
        for at in range(GROUPS * CAP):
            table_ref[at] = jnp.int32(-1)
        for i in range(SLOTS):
            doc = ids_ref[i % RETRIEVED, me * SERVED + i // RETRIEVED]
            location = home_ref[doc]
            at = location // STORED * CAP
            table_ref[at + jnp.where(table_ref[at] >= 0, 1, 0)] = jnp.int32(i)
            table_ref[GROUPS * CAP + i] = location % STORED
            table_ref[GROUPS * CAP + SLOTS + i] = len_ref[doc]

    copy_chosen(table_ref, cache_ref, EARLY, out_refs, *scratch, rest)


def second_pack_kernel(table_ref, cache_ref, *refs):
    out_refs, scratch = refs[: len(LATE)], refs[len(LATE) :]
    copy_chosen(table_ref, cache_ref, LATE, out_refs, *scratch, lambda: None)


def pack(kernel, blocks, scalars, cache, with_table):
    shapes = [(CAP * len(b), 2, DOC, HD) for b in blocks]
    total = sum(s[0] for s in shapes)
    table = [jax.ShapeDtypeStruct((CHOSEN + GROUPS * CAP + 1,), jnp.int32)] if with_table else []
    return pl.pallas_call(
        kernel,
        out_shape=[jax.ShapeDtypeStruct(s, jnp.bfloat16) for s in shapes] + table,
        in_specs=[SMEM] * len(scalars) + [HBM],
        out_specs=[HBM] * len(blocks) + [SMEM] * len(table),
        scratch_shapes=[
            pltpu.VMEM((total, 2, DOC, HD), jnp.bfloat16),
            pltpu.SemaphoreType.DMA((total,)),
            pltpu.SemaphoreType.DMA((total,)),
        ],
        compiler_params=pltpu.CompilerParams(vmem_limit_bytes=ALL_ROOM),
        cost_estimate=pl.CostEstimate(flops=0, bytes_accessed=5 << 20, transcendentals=0),
        name="pack",
    )(*scalars, cache)


def attend_kernel(shifts, count, first, last, *refs):
    refs = list(refs)
    table_ref, q_ref, pos_ref = refs[:3]
    if first:
        new_idx_ref, new_k_ref, new_v_ref = refs[3:6]
    arrays, refs = refs[6 : 6 + len(shifts)], refs[6 + len(shifts) :]
    acc, top_ref, sum_ref, *refs = refs
    if last:
        out_ref, *refs = refs
    buf, items, sem = refs
    me = table_ref[CHOSEN + GROUPS * CAP]
    x, y = me // SIDE, me % SIDE

    found = jnp.int32(0)
    for (dx, dy), array in zip(shifts, arrays):
        skip = CAP if (dx, dy) in JOINED else 0
        source = (x - dx + SIDE) % SIDE * SIDE + (y - dy + SIDE) % SIDE
        for k in range(CAP):
            i = table_ref[source * CAP + k]
            mine = i >= 0

            @pl.when(mine)
            def _(i=i, array=array, k=k, at=found, own=(dx, dy) == (0, 0)):
                where = table_ref[GROUPS * CAP + i] if own else k + skip
                items[at] = i
                pltpu.make_async_copy(array.at[where], buf.at[at], sem.at[at]).start()

            found = found + jnp.where(mine, 1, 0)

    def scores(r, tile, wide, keys, idx):
        q = []
        for n in range(wide):
            rows = pl.ds(pl.multiple_of((tile + n) * SUB, SUB), SUB)
            q += [q_ref[r, rows, h * HD : (h + 1) * HD] for h in range(GROUP)]
        s = lax.dot_general(
            jnp.concatenate(q, axis=0),
            keys,
            (((1,), (1,)), ((), ())),
            preferred_element_type=jnp.float32,
        )
        pos = pos_ref[r, pl.ds(tile, wide)].reshape(wide * ROWS, 1)
        return jnp.where(idx <= pos, s, -1e30)

    def weigh(s, top):
        p = jnp.exp2((s - jnp.concatenate([top] * (s.shape[1] // HD), axis=1)) * EXP2)
        parts = [p[:, c : c + HD] for c in range(0, s.shape[1], HD)]
        return p.astype(jnp.bfloat16), functools.reduce(jnp.add, parts)

    def put(ref, r, tile, wide, value):
        ref[r, pl.ds(tile, wide)] = value.reshape(wide, ROWS, HD)

    if first:

        def start(at, carry):
            r, tile = at // (TILES // 2), at % (TILES // 2) * 2
            s = scores(r, tile, 2, new_k_ref[r], new_idx_ref[r])
            top = jnp.broadcast_to(jnp.max(s, axis=1, keepdims=True), (2 * ROWS, HD))
            p, sums = weigh(s, top)
            put(top_ref, r, tile, 2, top)
            put(sum_ref, r, tile, 2, sums)
            value = jnp.dot(p, new_v_ref[r], preferred_element_type=jnp.float32)
            put(acc, r, tile, 2, value)
            return carry

        lax.fori_loop(0, count * TILES // 2, start, 0)

    def item(at, carry):
        i = items[at]
        r, j = i // RETRIEVED, i % RETRIEVED
        length = table_ref[GROUPS * CAP + SLOTS + i]
        row = lax.broadcasted_iota(jnp.int32, (1, DOC), 1)
        idx = row + j * DOC
        per = RETRIEVED // TILES
        picked = pos_ref[r, j // per, pl.ds(pl.multiple_of(j % per * PICK, PICK), PICK)]
        replaced = jnp.max(jnp.where(picked == idx, 1, 0), axis=0, keepdims=True)
        idx = jnp.where((row < length) & (replaced == 0), idx, FAR)
        pltpu.make_async_copy(arrays[0].at[0], buf.at[at], sem.at[at]).wait()

        bias = jnp.where(idx < FAR, 0.0, -1e30)

        def step(tile):
            wide = TILES - tile

            def get(ref):
                return ref[r, tile:].reshape(wide * ROWS, HD)

            q = []
            for n in range(tile, TILES):
                rows = slice(n * SUB, (n + 1) * SUB)
                q += [q_ref[r, rows, h * HD : (h + 1) * HD] for h in range(GROUP)]
            s = lax.dot_general(
                jnp.concatenate(q, axis=0),
                buf[at, 0],
                (((1,), (1,)), ((), ())),
                preferred_element_type=jnp.float32,
            )
            within = jnp.where(idx <= pos_ref[r, tile], s[:ROWS], -1e30)
            s = jnp.concatenate([within, s[ROWS:] + bias], axis=0) if wide > 1 else within
            before = get(top_ref)
            top = jnp.maximum(before, jnp.max(s, axis=1, keepdims=True))
            fade = jnp.exp2((before - top) * EXP2)
            p, sums = weigh(s, top)
            value = jnp.dot(p, buf[at, 1], preferred_element_type=jnp.float32)
            shape = (wide, ROWS, HD)
            top_ref[r, tile:] = top.reshape(shape)
            sum_ref[r, tile:] = (get(sum_ref) * fade + sums).reshape(shape)
            acc[r, tile:] = (get(acc) * fade + value).reshape(shape)

        for tile in range(TILES):
            pl.when(j // per == tile)(functools.partial(step, tile))
        return carry

    lax.fori_loop(0, found, item, 0)

    if last:
        for r in range(count):
            for tile in range(TILES):
                sums = jnp.sum(sum_ref[r, tile], axis=1, keepdims=True)
                done = (acc[r, tile] / sums).astype(jnp.bfloat16)
                rows = slice(r * TOKENS + tile * SUB, r * TOKENS + (tile + 1) * SUB)
                for h in range(GROUP):
                    out_ref[rows, h * HD : (h + 1) * HD] = done[h * SUB : (h + 1) * SUB]


def attend(table, query, pos, extra, arrays, shifts, first, last):
    cands, count = CAP * len(arrays), query.shape[0]

    state = jax.ShapeDtypeStruct((count, TILES, ROWS, HD), jnp.float32)
    out_shape = [state] * 3
    if last:
        out_shape.append(jax.ShapeDtypeStruct((count * TOKENS, GROUP * HD), jnp.bfloat16))
    return pl.pallas_call(
        functools.partial(attend_kernel, shifts, count, first, last),
        out_shape=out_shape,
        in_specs=[SMEM] + [VMEM] * 5 + [ANY] * len(arrays),
        out_specs=[VMEM] * len(out_shape),
        scratch_shapes=[
            pltpu.VMEM((cands, 2, DOC, HD), jnp.bfloat16),
            pltpu.SMEM((cands,), jnp.int32),
            pltpu.SemaphoreType.DMA((cands,)),
        ],
        input_output_aliases={} if first else {3: 0, 4: 1, 5: 2},
        compiler_params=pltpu.CompilerParams(vmem_limit_bytes=ROOM),
        cost_estimate=pl.CostEstimate(
            flops=count * 2 * 1280 * 512 * 128 * len(arrays),
            bytes_accessed=count * ((4 << 20) + len(arrays) * (1 << 17)),
            transcendentals=count * 1280 * 512 * len(arrays) // 2,
        ),
        name="attend",
    )(table, query, pos, *extra, *arrays)


def project_kernel(spans, last, place_ref, w_ref, *refs):
    parts, refs = refs[: len(spans)], refs[len(spans) :]
    if last:
        before_ref, *refs = refs
    out_ref = refs[0]
    width = GROUP * HD
    rows = out_ref.shape[0]
    half = rows // 2
    for at in range(0, rows, half):
        total = before_ref[at : at + half] if last else None
        for part, (n, lo, hi) in zip(parts, spans):
            if lo <= at < hi:
                block = pl.ds(pl.multiple_of(place_ref[n] * width, width), width)
                term = jnp.dot(
                    part[at - lo : at - lo + half],
                    w_ref[block, :],
                    preferred_element_type=jnp.float32,
                )
                total = term if total is None else total + term
        out_ref[at : at + half] = total.astype(out_ref.dtype)


def project(place, pieces, w_out, before):
    spans, parts = [p[:3] for p in pieces], [p[3] for p in pieces]
    rows, columns = max(hi for _, _, hi in spans), w_out.shape[1]
    blocks, last = len({n for n, _, _ in spans}), before is not None
    return pl.pallas_call(
        functools.partial(project_kernel, spans, last),
        out_shape=jax.ShapeDtypeStruct((rows, columns), jnp.bfloat16 if last else jnp.float32),
        in_specs=[SMEM] + [VMEM] * (len(parts) + 1 + last),
        out_specs=VMEM,
        compiler_params=pltpu.CompilerParams(vmem_limit_bytes=PROJECT_ROOM),
        cost_estimate=pl.CostEstimate(
            flops=2 * rows * blocks * 512 * 512, bytes_accessed=blocks << 20, transcendentals=0
        ),
        name="project",
    )(place, w_out, *parts, *([before] if last else []))


def ring(block, by):
    return lax.ppermute(block, "tp", [(i, (i + 2 * by) % KVH) for i in range(KVH)])


def other_core(block):
    return lax.ppermute(block, "tp", [(i, i ^ 1) for i in range(KVH)])


def body(
    sel_hidden,
    norm_gain,
    w_query,
    w_key,
    w_value,
    w_out,
    doc_cache,
    home,
    doc_ids,
    doc_len,
    positions,
):
    me = lax.axis_index("grp").astype(jnp.int32).reshape(1)
    served = sel_hidden.shape[0]

    with jax.named_scope("pack"):
        scalars = [me, home, doc_ids.T, doc_len]
        *early, table = pack(first_pack_kernel, EARLY, scalars, doc_cache, True)
        late = list(pack(second_pack_kernel, LATE, [table], doc_cache, False))
        packed = {b[0]: p for b, p in zip(EARLY + LATE, early + late)}

    with jax.named_scope("positions"):
        new_index = jnp.pad(
            positions, ((0, 0), (0, PADDED - TOKENS)), constant_values=FAR
        ).reshape(served, 1, PADDED)
        row_pos = jnp.broadcast_to(
            positions.reshape(served, TILES, 1, SUB), (served, TILES, GROUP, SUB)
        ).reshape(served, TILES, ROWS, 1)

    with jax.named_scope("projections"):
        xf = sel_hidden.astype(jnp.float32)
        normed = (
            xf * lax.rsqrt(jnp.mean(xf * xf, axis=-1, keepdims=True) + 1e-05) * norm_gain
        ).astype(jnp.bfloat16)
        normed_rows = normed.reshape(served * TOKENS, normed.shape[2])

        def dot(w):
            out = jnp.dot(normed_rows, w, preferred_element_type=jnp.float32)
            return out.astype(jnp.bfloat16).reshape(served, TOKENS, w.shape[1])

        query, key_new, value_new = dot(w_query), dot(w_key), dot(w_value)
        pad = ((0, 0), (0, PADDED - TOKENS), (0, 0))
        key_new, value_new = jnp.pad(key_new, pad), jnp.pad(value_new, pad)

    arrived = {(0, 0): doc_cache}

    def after(blocks, *done):
        return lax.optimization_barrier((blocks, done))[0]

    def send(names, blocks, hops):
        with jax.named_scope("documents"):
            for s, block, hop in zip(names, blocks, hops):
                arrived[s] = shift(block, hop)

    def attention(n, state):
        shifts, last = STAGES[n], n == len(STAGES) - 1
        with jax.named_scope("attention"):
            return attend(
                table,
                query,
                row_pos,
                state,
                [arrived[s] for s in shifts],
                shifts,
                n == 0,
                last,
            )

    send(TWO, [packed[s] for s in TWO], TWO)
    send(DIAGONAL, [packed[s] for s in DIAGONAL], DIAGONAL)
    state = attention(0, [new_index, key_new, value_new])
    now = NEAR + OPPOSITE
    send(now, after([packed[s] for s in now], [arrived[s] for s in TWO], state), now)
    blocks = []
    for s in KNIGHT:
        through = (0, 2) if s[1] == 2 else (2, 0)
        at = CAP * CARRIED[through].index(s)
        blocks.append(arrived[through][at : at + CAP])
    send(KNIGHT[:1], after(blocks[:1], [arrived[s] for s in DIAGONAL], state), NEAR[:1])
    state = attention(1, state)
    send(KNIGHT[1:], after(blocks[1:], state), NEAR[1:])
    state = attention(2, state)
    own = attention(len(STAGES) - 1, state)[-1]

    with jax.named_scope("output"):
        tp = lax.axis_index("tp")
        z, core = tp // 2, tp % 2
        planes = jnp.stack([z, (z + 3) % SIDE, (z + 1) % SIDE, (z + 2) % SIDE])
        place = jnp.concatenate([planes * 2 + core, planes * 2 + 1 - core]).astype(jnp.int32)
        rows = served * TOKENS
        half = rows // 2
        up, down, core = ring(own, 1), ring(own, -1), other_core(own)
        near = [(0, own), (4, core), (1, up), (2, down), (5, other_core(up)), (6, other_core(down))]
        near = [(n, 0, rows, p) for n, p in near]
        far = [ring(up[:half], 1), ring(down[half:], -1)]
        partial = project(place, near, w_out, None)
        far = lax.optimization_barrier((far, partial))[0]
        cross = [other_core(p) for p in far]
        pieces = [(3, 0, half, far[0]), (3, half, rows, far[1])]
        pieces += [(7, 0, half, cross[0]), (7, half, rows, cross[1])]
        mixed = project(place, pieces, w_out, partial)
        return mixed.reshape(served, TOKENS, w_out.shape[1])


def solution(mesh):
    return jax.shard_map(
        body,
        mesh=mesh,
        in_specs=(
            P("grp", None, None),
            P(),
            P(None, "tp"),
            P(None, "tp"),
            P(None, "tp"),
            P(None, "tp"),
            P("grp", None, None, "tp"),
            P(),
            P(),
            P(),
            P("grp", None),
        ),
        out_specs=P("grp", None, "tp"),
        check_vma=False,
    )
```
